32 devices in a mesh: chan: 4 (over y, x), head: 4 (over z), region: 2 (over core).
Axes of the slice: x: 2, y: 2, z: 4, core: 2. Of those that a mesh axis runs over, the one named last changes fastest.
Arguments:
- tokens: bfloat16 [64, 16, 4096], P('chan', 'region', 'head'), parts along dimension 1, may hold values from -56 to 56
- position: bfloat16 [64, 4096], P('chan', 'head'), may hold values from -3 to 3
- gain: bfloat16 [4096], P('head'), may hold values from 0.099609375 to 1.8984375
- qkv_weight: bfloat16 [3, 4096, 2048], P(None, 'chan', 'head'), may hold values from -0.09375 to 0.09375
- out_weight: bfloat16 [2048, 4096], P('head'), may hold values from -0.25 to 0.25
- cotangent: bfloat16 [64, 16, 4096], P('chan', 'region', 'head'), parts along dimension 1, may hold values from -6 to 6
Outputs:
- layer_out: bfloat16 [64, 16, 4096], P('chan', 'region', 'head'), parts along dimension 1
- input_grad: bfloat16 [64, 16, 4096], P('chan', 'region', 'head'), parts along dimension 1
The draws below stay inside these ranges and needn't reach their ends.
There are 2 independent parts, one for each index of `region`. The reference program is written for one: setup_inputs(seed, part) draws one part's arguments, and reference() takes and returns one part's arrays. A program takes and returns all parts, laid end to end along the dimension named above; an argument that names none is the same for every part. Nothing has to cross between parts.
All inputs are finite; a program needn't handle non-finite values.
Results may differ from the reference program's by a relative error of at most 0.01.
Values may be sent and summed in bfloat16 or wider, within the bound.
A program may use at most 64 MiB of HBM per device.

```python
import math
import jax
import jax.numpy as jnp
from jax import lax

D = 4096
HEADS_W = 16
HDIM = 128
CHG = 16
PATCH = 8
HF = 2048
CHANNELS = 64
N_CHAN = 4


def draw_tokens(key, part):
    key_pattern, key_columns, key_rows = jax.random.split(key, 3)
    array_shape = (CHANNELS, PATCH, D)
    column_frac = jnp.arange(D, dtype=jnp.float32) / D
    rising = jnp.exp(math.log(3.0) * (column_frac - 0.5))
    pattern = jnp.clip(jax.random.normal(key_pattern, array_shape, jnp.float32), -4.0, 4.0)
    columns = jnp.exp(jax.random.uniform(key_columns, (D,), jnp.float32, math.log(0.3), math.log(3.0)))
    row_scale = jnp.exp(jax.random.uniform(key_rows, (CHANNELS, PATCH, 1), jnp.float32, math.log(0.5), math.log(2.0)))
    return (pattern * columns * rising * row_scale).astype(jnp.bfloat16)


def shard_levels(key, extent, cuts, low, largest):
    def one(dim, shards_of):
        heights = jax.random.uniform(jax.random.fold_in(jax.random.fold_in(key, 6), dim), (shards_of,), jnp.float32, low / len(cuts), largest / len(cuts))
        return jnp.repeat(jnp.exp(heights), extent[dim] // shards_of).reshape((-1,) + (1,) * (len(extent) - dim - 1))

    factor_of = one(*cuts[0])
    for cut in cuts[1:]:
        factor_of = factor_of * one(*cut)
    return factor_of


def normal_values(key, extent, spread, bound, pieces=(), kind=jnp.bfloat16):
    level = shard_levels(key, extent, pieces, -0.22, 0.18) if pieces else 1.0
    drawn = jax.random.normal(key, extent, jnp.float32) * spread * level
    return jnp.minimum(jnp.maximum(drawn, -bound), bound).astype(kind)


def setup_inputs(seed: int = 0, part: int = 0) -> dict:
    seeds = jax.random.split(jax.random.key(seed), 7)
    part_keys = jax.random.split(jax.random.fold_in(seeds[6], part), 7)
    return {
        "tokens": draw_tokens(jax.random.fold_in(jax.random.fold_in(seeds[6], part), 71), part),
        "position": normal_values(seeds[1], (CHANNELS, D), 0.5, 3.0, ((0, 4), (1, 4))),
        "gain": jnp.clip(1.0 + 0.18 * jax.random.normal(seeds[2], (D,), jnp.float32), 0.099609375, 1.8984375).astype(jnp.bfloat16),
        "qkv_weight": normal_values(seeds[3], (3, D, HF), D ** -0.5, 0.09375, ((1, 4), (2, 4))),
        "out_weight": normal_values(seeds[4], (HF, D), (HF // 4) ** -0.5, 0.25, ((0, 4),)),
        "cotangent": normal_values(part_keys[5], (CHANNELS, PATCH, D), 1.0, 6.0, ((0, 4), (2, 4))),
    }


def head_norm(values):
    return values * lax.rsqrt(lax.optimization_barrier(jnp.mean(values * values, axis=-1, keepdims=True)) + 1e-06)

def within_group(queries, keys_in, values):
    factor = queries.shape[-1] ** (-0.5)
    scores = jnp.einsum('cpne,dpne->pncd', head_norm(queries), head_norm(keys_in)) * factor
    weights = jnp.exp(scores)
    weights = weights / lax.optimization_barrier(jnp.sum(weights, axis=-1, keepdims=True))
    return jnp.einsum('pncd,dpne->cpne', weights, values)

def across_groups(queries, aggregates):
    factor = queries.shape[-1] ** (-0.5)
    scores = jnp.einsum('cpne,gpne->cpng', head_norm(queries), head_norm(aggregates)) * factor
    weights = jnp.exp(scores)
    weights = weights / lax.optimization_barrier(jnp.sum(weights, axis=-1, keepdims=True))
    return jnp.einsum('cpng,gpne->cpne', weights, aggregates)

def reference(tokens, position, gain, qkv_weight, out_weight, cotangent):
    groups = N_CHAN
    channels, patches, width = tokens.shape
    row_count = channels * patches
    hidden_in = (tokens.astype(jnp.float32) + position[:, None, :].astype(jnp.float32)).astype(jnp.bfloat16)
    hidden_f = hidden_in.astype(jnp.float32)
    inv_rms = lax.rsqrt(lax.optimization_barrier(jnp.mean(hidden_f * hidden_f, axis=-1, keepdims=True)) + 1e-05)
    gain_f = gain.astype(jnp.float32)
    normed = (hidden_f * inv_rms * gain_f).astype(jnp.bfloat16).reshape(row_count, width)
    projected = []
    for index in range(3):
        product = jnp.dot(normed, qkv_weight[index], preferred_element_type=jnp.float32)
        product = lax.optimization_barrier(product.astype(jnp.bfloat16)).astype(jnp.float32)
        projected.append(product.reshape(groups, CHG, patches, HEADS_W, HDIM))
    queries, keys_in, values = projected
    first = jax.vmap(within_group)(queries, keys_in, values)
    aggregates = lax.optimization_barrier(jnp.mean(first, axis=1))
    aggregates = lax.optimization_barrier(aggregates.astype(jnp.bfloat16)).astype(jnp.float32)
    queries_flat = queries.reshape(channels, patches, HEADS_W, HDIM)
    second = across_groups(queries_flat, aggregates)
    mixed = (first.reshape(channels, patches, HEADS_W, HDIM) + second).astype(jnp.bfloat16).reshape(row_count, HF)
    branch_out = jnp.dot(mixed, out_weight, preferred_element_type=jnp.float32).reshape(channels, patches, width)
    layer_out = (hidden_f + branch_out).astype(jnp.bfloat16)
    grad_mixed = lax.dot_general(cotangent.reshape(row_count, width), out_weight, (((1,), (1,)), ((), ())), preferred_element_type=jnp.float32)
    grad_mixed = grad_mixed.reshape(channels, patches, HEADS_W, HDIM)
    unused_second, back_across = jax.vjp(across_groups, queries_flat, aggregates)
    grad_q_second, grad_aggregates = back_across(grad_mixed)
    grad_first = grad_mixed.reshape(groups, CHG, patches, HEADS_W, HDIM) + grad_aggregates[:, None] / CHG
    unused_first, back_within = jax.vjp(jax.vmap(within_group), queries, keys_in, values)
    grad_q, grad_k, grad_v = back_within(grad_first)
    grad_q = grad_q.reshape(channels, patches, HEADS_W, HDIM) + grad_q_second
    rounded = [grad_q.astype(jnp.bfloat16), grad_k.astype(jnp.bfloat16), grad_v.astype(jnp.bfloat16)]
    grad_normed = jnp.zeros((row_count, width), jnp.float32)
    for index in range(3):
        grad_normed = grad_normed + lax.dot_general(rounded[index].reshape(row_count, HF), qkv_weight[index], (((1,), (1,)), ((), ())), preferred_element_type=jnp.float32)
    grad_normed = grad_normed.reshape(channels, patches, width)
    correction = lax.optimization_barrier(jnp.mean(hidden_f * gain_f * grad_normed, axis=-1, keepdims=True))
    grad_hidden = inv_rms * gain_f * grad_normed - hidden_f * inv_rms * inv_rms * inv_rms * correction
    input_grad = (cotangent.astype(jnp.float32) + grad_hidden).astype(jnp.bfloat16)
    return (layer_out, input_grad)
```

```python
import functools

import jax
import jax.numpy as jnp
from jax import lax
from jax.experimental import pallas as pl
from jax.experimental.pallas import tpu as pltpu
from jax.sharding import PartitionSpec as P

HDIM = 128
MESH = pl.DeviceIdType.MESH
F32 = jnp.float32
BF16 = jnp.bfloat16

NN = (((1,), (0,)), ((), ()))
NT = (((1,), (1,)), ((), ()))
TN = (((0,), (0,)), ((), ()))


def mm(a, b, dims):
    return lax.dot_general(a, b, dims, preferred_element_type=F32)


def unit(u):
    r = lax.rsqrt(jnp.mean(u * u, axis=-1, keepdims=True) + 1e-06)
    return u * r, r


def unit_back(y, r, dy):
    return r * (dy - y * jnp.mean(y * dy, axis=-1, keepdims=True))


def same_patch(rows, columns, patches):
    a = lax.broadcasted_iota(jnp.int32, (rows, columns), 0)
    b = lax.broadcasted_iota(jnp.int32, (rows, columns), 1)
    return (a % patches == b % patches).astype(F32)


def softmax(a, b, mask):
    w = jnp.exp(mm(a.astype(BF16), b.astype(BF16), NT) * HDIM ** (-0.5)) * mask
    return w / jnp.sum(w, axis=-1, keepdims=True)


def kernel(
    C, H, R, patches,
    hid, cot, gain8, qkv, ow, lay_ref, inp_ref,
    wall, wo, hall, call, gall, normed, inv, proj, gm, wts, aggs, gq2, gsend, grecv,
    grads, s1, r1, s2, r2, own1, own2, corr, rcorr,
    loc, wsnd, wrcv, hs, hr, cs, cr, gs, gr, as_, ar, gas, gar, s1s, s1r, s2s, s2r, ks, kr,
):
    c, h, r = lax.axis_index("chan"), lax.axis_index("head"), lax.axis_index("region")
    T, W = hid.shape
    S, F = qkv.shape[1], qkv.shape[2]
    heads = F // HDIM
    chg = T // patches
    square = C == 4 and R == 2
    half = S // 2

    def remote(src, dst, ss, rs, **where):
        return pltpu.make_async_remote_copy(
            src_ref=src, dst_ref=dst, send_sem=ss, recv_sem=rs, device_id=where, device_id_type=MESH
        )

    barrier = pltpu.get_barrier_semaphore()
    for k in range(1, C):
        pl.semaphore_signal(barrier, inc=1, device_id={"chan": lax.rem(c + k, C)}, device_id_type=MESH)
    for k in range(1, H):
        pl.semaphore_signal(barrier, inc=1, device_id={"head": lax.rem(h + k, H)}, device_id_type=MESH)
    extra = 0
    if square:
        extra = 1
        pl.semaphore_signal(barrier, inc=1, device_id={"region": 1 - r}, device_id_type=MESH)

    own_w = pltpu.make_async_copy(qkv, wall.at[:, pl.ds(pl.multiple_of(c * S, S), S)], loc.at[0])
    own_w.start()
    own_o = []
    for i in range(H):
        cp = pltpu.make_async_copy(ow.at[:, pl.ds(i * W, W)], wo.at[i], loc.at[1 + i])
        cp.start()
        own_o.append(cp)
    pl.semaphore_wait(barrier, C - 1 + H - 1 + extra)

    sent = []

    def to_heads(src, buf, ss, rs):
        for k in range(1, H):
            cp = remote(src, buf.at[h], ss.at[k - 1], rs.at[k - 1], head=lax.rem(h + k, H))
            cp.start()
            sent.append(cp)

    def from_heads(buf, ss, rs):
        for k in range(1, H):
            slot = buf.at[lax.rem(h + H - k, H)]
            remote(slot, slot, ss.at[k - 1], rs.at[k - 1], head=lax.rem(h + k, H)).wait_recv()

    def rows_of(j, block, part):
        return wall.at[j, pl.ds(pl.multiple_of(block * S + part * half, half), half)]

    if square:
        y, x = c // 2, c % 2
        xn, yn, dg = y * 2 + 1 - x, (1 - y) * 2 + x, (1 - y) * 2 + 1 - x
        near = (xn * (1 - r) + yn * r, yn * (1 - r) + xn * r)
        mate_near = (near[1], near[0])
        blocks = (near[0], near[1], dg)
        mate_blocks = (mate_near[0], mate_near[1], dg)

        def put(slot, j, src, block, part, **where):
            i = slot * 3 + j
            cp = remote(src, rows_of(j, block, part), wsnd.at[i], wrcv.at[i], **where)
            cp.start()
            sent.append(cp)

        def took(slot, j):
            i = slot * 3 + j
            if slot < 3:
                ref = rows_of(j, blocks[slot], r)
            else:
                ref = rows_of(j, mate_blocks[slot - 3], 1 - r)
            remote(ref, ref, wsnd.at[i], wrcv.at[i], region=1 - r).wait_recv()

        def pass_on(slot, j):
            took(slot, j)
            src = rows_of(j, blocks[slot], r)
            if slot == 0:
                put(2, j, src, blocks[0], r, chan=near[1])
            put(3 + slot, j, src, blocks[slot], r, region=1 - r)

    to_heads(hid, hall, hs, hr)
    to_heads(gain8, gall, gs, gr)
    if square:
        for j in range(3):
            src = qkv.at[j, pl.ds(pl.multiple_of(r * half, half), half)]
            put(0, j, src, c, r, chan=near[0])
            put(1, j, src, c, r, chan=near[1])
    else:
        mine = pl.ds(pl.multiple_of(c * S, S), S)
        for k in range(1, C):
            cp = remote(qkv, wall.at[:, mine], wsnd.at[k - 1], wrcv.at[k - 1], chan=lax.rem(c + k, C))
            cp.start()
            sent.append(cp)
    to_heads(cot, call, cs, cr)
    hall[h] = hid[...]
    call[h] = cot[...]
    gall[h] = gain8[...]

    if square:
        pass_on(0, 0)
        pass_on(1, 0)

    from_heads(hall, hs, hr)
    from_heads(gall, gs, gr)
    total = jnp.zeros((T, 1), F32)
    for i in range(H):
        b = hall[i].astype(F32)
        total += jnp.sum(b * b, axis=-1, keepdims=True)
    scale = lax.rsqrt(total / (H * W) + 1e-05)
    inv[...] = jnp.broadcast_to(scale, inv.shape)

    def norm_block(i, carry):
        normed[i] = (hall[i].astype(F32) * inv[:, :1] * gall[i][:1, :]).astype(BF16)
        return carry

    lax.fori_loop(0, H, norm_block, 0)

    if square:
        for j in (1, 2):
            pass_on(0, j)
            pass_on(1, j)

    for cp in own_o:
        cp.wait()
    from_heads(call, cs, cr)
    gm[...] = jnp.zeros_like(gm)

    def mixed_block(i, carry):
        gm[...] += mm(call[i], wo[i], NT)
        return carry

    lax.fori_loop(0, H, mixed_block, 0)

    own_w.wait()
    if square:
        for j in range(3):
            pass_on(2, j)
    else:
        for k in range(1, C):
            ref = wall.at[:, pl.ds(pl.multiple_of(lax.rem(c + C - k, C) * S, S), S)]
            remote(ref, ref, wsnd.at[k - 1], wrcv.at[k - 1], chan=lax.rem(c + k, C)).wait_recv()
    for j in range(3):
        if square:
            for slot in (3, 4, 5):
                took(slot, j)
        own1[:, :F] = jnp.zeros((T, F), F32)

        def project(i, carry):
            own1[:, :F] += mm(normed[i], wall[j, pl.ds(pl.multiple_of(i * W, W), W), :], NN)
            return carry

        lax.fori_loop(0, H, project, 0)
        proj[j] = own1[:, :F].astype(BF16)

    mask = same_patch(T, T, patches)
    for n in range(heads):
        cols = slice(n * HDIM, (n + 1) * HDIM)
        qn, _ = unit(proj[0][:, cols].astype(F32))
        kn, _ = unit(proj[1][:, cols].astype(F32))
        w = softmax(qn, kn, mask)
        wts[n] = w
        first = mm(w.astype(BF16), proj[2][:, cols], NN)
        own2[:, cols] = first
        mean = jnp.mean(first.reshape(chg, patches, HDIM), axis=0)
        own1[:patches, cols] = mean.astype(BF16).astype(F32)
    aggs[c] = own1[:patches, :F]

    def to_groups(src_of, buf, ss, rs):
        for k in range(1, C):
            peer = lax.rem(c + k, C)
            cp = remote(src_of(peer), buf.at[c], ss.at[k - 1], rs.at[k - 1], chan=peer)
            cp.start()
            sent.append(cp)

    def from_groups(buf, ss, rs):
        for k in range(1, C):
            slot = buf.at[lax.rem(c + C - k, C)]
            remote(slot, slot, ss.at[k - 1], rs.at[k - 1], chan=lax.rem(c + k, C)).wait_recv()

    to_groups(lambda peer: aggs.at[c], aggs, as_, ar)
    from_groups(aggs, as_, ar)

    mask2 = same_patch(T, C * patches, patches)
    for n in range(heads):
        cols = slice(n * HDIM, (n + 1) * HDIM)
        a = aggs[:, :, cols].reshape(C * patches, HDIM)
        a16 = a.astype(BF16)
        qn, rq = unit(proj[0][:, cols].astype(F32))
        an, ra = unit(a)
        w = softmax(qn, an, mask2)
        w16 = w.astype(BF16)
        own2[:, cols] += mm(w16, a16, NN)
        g16 = gm[:, cols].astype(BF16)
        dw = mm(g16, a16, NT)
        ds = w * (dw - jnp.sum(w * dw, axis=-1, keepdims=True)) * HDIM ** (-0.5)
        ds16 = ds.astype(BF16)
        gq2[:, cols] = unit_back(qn, rq, mm(ds16, an.astype(BF16), NN))
        da = mm(w16, g16, TN) + unit_back(an, ra, mm(ds16, qn.astype(BF16), TN))
        gsend[:, :, cols] = da.reshape(C, patches, HDIM)
    to_groups(lambda peer: gsend.at[peer], grecv, gas, gar)
    grecv[c] = gsend[c]

    mixed = own2[:, :F].astype(BF16)
    for k in range(1, H):
        peer = lax.rem(h + k, H)
        s1[k - 1] = mm(mixed, wo[peer], NN).astype(BF16)
        cp = remote(s1.at[k - 1], r1.at[k - 1], s1s.at[k - 1], s1r.at[k - 1], head=peer)
        cp.start()
        sent.append(cp)
    own1[...] = mm(mixed, wo[h], NN)

    from_groups(grecv, gas, gar)
    back = grecv[0]
    for i in range(1, C):
        back = back + grecv[i]
    back = back / chg

    for n in range(heads):
        cols = slice(n * HDIM, (n + 1) * HDIM)
        lift = jnp.broadcast_to(back[None, :, cols], (chg, patches, HDIM)).reshape(T, HDIM)
        g16 = (gm[:, cols] + lift).astype(BF16)
        qn, rq = unit(proj[0][:, cols].astype(F32))
        kn, rk = unit(proj[1][:, cols].astype(F32))
        w = wts[n]
        dw = mm(g16, proj[2][:, cols], NT)
        ds = w * (dw - jnp.sum(w * dw, axis=-1, keepdims=True)) * HDIM ** (-0.5)
        ds16 = ds.astype(BF16)
        dq = unit_back(qn, rq, mm(ds16, kn.astype(BF16), NN)) + gq2[:, cols]
        dk = unit_back(kn, rk, mm(ds16, qn.astype(BF16), TN))
        grads[0, :, cols] = dq.astype(BF16)
        grads[1, :, cols] = dk.astype(BF16)
        grads[2, :, cols] = mm(w.astype(BF16), g16, TN).astype(BF16)

    dots = jnp.zeros((T, 1), F32)
    for k in list(range(1, H)) + [0]:
        peer = lax.rem(h + k, H)
        own2[...] = jnp.zeros_like(own2)

        def back_proj(j, carry):
            own2[...] += mm(grads[j], wall[j, pl.ds(pl.multiple_of(peer * W, W), W), :], NT)
            return carry

        lax.fori_loop(0, 3, back_proj, 0)
        if k:
            s2[k - 1] = own2[...].astype(BF16)
            cp = remote(s2.at[k - 1], r2.at[k - 1], s2s.at[k - 1], s2r.at[k - 1], head=peer)
            cp.start()
            sent.append(cp)
        dots += jnp.sum(hall[peer].astype(F32) * gall[peer][:1, :] * own2[...], axis=-1, keepdims=True)
    corr[...] = jnp.broadcast_to(dots, corr.shape)
    for k in range(1, H):
        cp = remote(corr, rcorr.at[k - 1], ks.at[k - 1], kr.at[k - 1], head=lax.rem(h + k, H))
        cp.start()
        sent.append(cp)

    def from_shares(buf, ss, rs, k):
        slot = buf.at[k - 1]
        remote(slot, slot, ss.at[k - 1], rs.at[k - 1], head=lax.rem(h + k, H)).wait_recv()

    for k in range(1, H):
        from_shares(r1, s1s, s1r, k)
        own1[...] += r1[k - 1].astype(F32)
    lay_ref[...] = (hid[...].astype(F32) + own1[...]).astype(BF16)
    for k in range(1, H):
        from_shares(r2, s2s, s2r, k)
        own2[...] += r2[k - 1].astype(F32)
    for k in range(1, H):
        from_shares(rcorr, ks, kr, k)
        corr_k = rcorr[k - 1]
        dots += corr_k[:, :1]
    ir = inv[:, :1]
    grad = ir * gain8[:1, :] * own2[...] - hid[...].astype(F32) * (ir * ir * ir * dots / (H * W))
    inp_ref[...] = (cot[...].astype(F32) + grad).astype(BF16)
    for cp in sent:
        cp.wait_send()


def per_device(C, H, R, tokens, position, gain, qkv_weight, out_weight, cotangent):
    channels, patches, W = tokens.shape
    T = channels * patches
    hidden = (tokens.astype(F32) + position[:, None, :].astype(F32)).astype(BF16).reshape(T, W)
    cot = cotangent.reshape(T, W)
    gain8 = jnp.broadcast_to(gain.astype(F32)[None, :], (8, W))
    S, F = qkv_weight.shape[1:]
    heads = F // HDIM
    D = S * C
    V = pltpu.VMEM
    dma = lambda n: pltpu.SemaphoreType.DMA((n,))
    nw = 18 if (C == 4 and R == 2) else C - 1
    z, g = H - 1, C - 1
    vm = pl.BlockSpec(memory_space=pltpu.VMEM)
    hbm = pl.BlockSpec(memory_space=pl.ANY)
    lay, inp = pl.pallas_call(
        functools.partial(kernel, C, H, R, patches),
        out_shape=[jax.ShapeDtypeStruct((T, W), BF16)] * 2,
        in_specs=[vm, vm, vm, hbm, hbm],
        out_specs=[vm, vm],
        scratch_shapes=[
            V((3, D, F), BF16), V((H, F, W), BF16), V((H, T, W), BF16), V((H, T, W), BF16),
            V((H, 8, W), F32), V((H, T, W), BF16), V((T, HDIM), F32), V((3, T, F), BF16),
            V((T, F), F32), V((heads, T, T), F32), V((C, patches, F), F32), V((T, F), F32),
            V((C, patches, F), F32), V((C, patches, F), F32), V((3, T, F), BF16),
            V((z, T, W), BF16), V((z, T, W), BF16), V((z, T, W), BF16), V((z, T, W), BF16),
            V((T, W), F32), V((T, W), F32), V((T, HDIM), F32), V((z, T, HDIM), F32),
            dma(1 + H), dma(nw), dma(nw), dma(z), dma(z), dma(z), dma(z), dma(z), dma(z),
            dma(g), dma(g), dma(g), dma(g), dma(z), dma(z), dma(z), dma(z), dma(z), dma(z),
        ],
        compiler_params=pltpu.CompilerParams(
            collective_id=0, has_side_effects=True, vmem_limit_bytes=50 * 1024 * 1024
        ),
    )(hidden, cot, gain8, qkv_weight, out_weight)
    return lay.reshape(channels, patches, W), inp.reshape(channels, patches, W)


def solution(mesh):
    C, H, R = (mesh.shape[a] for a in ("chan", "head", "region"))
    return jax.shard_map(
        functools.partial(per_device, C, H, R),
        mesh=mesh,
        in_specs=(
            P("chan", "region", "head"),
            P("chan", "head"),
            P("head"),
            P(None, "chan", "head"),
            P("head", None),
            P("chan", "region", "head"),
        ),
        out_specs=(P("chan", "region", "head"), P("chan", "region", "head")),
        check_vma=False,
    )
```

```python
import functools

import jax
import jax.numpy as jnp
from jax import lax
from jax.experimental import pallas as pl
from jax.experimental.pallas import tpu as pltpu
from jax.sharding import PartitionSpec as P

HDIM = 128
MESH = pl.DeviceIdType.MESH
F32 = jnp.float32
BF16 = jnp.bfloat16

NN = (((1,), (0,)), ((), ()))
NT = (((1,), (1,)), ((), ()))
TN = (((0,), (0,)), ((), ()))


def mm(a, b, dims):
    return lax.dot_general(a, b, dims, preferred_element_type=F32)


def unit(u):
    r = lax.rsqrt(jnp.mean(u * u, axis=-1, keepdims=True) + 1e-06)
    return u * r, r


def unit_back(y, r, dy):
    return r * (dy - y * jnp.mean(y * dy, axis=-1, keepdims=True))


def same_patch(rows, columns, patches):
    a = lax.broadcasted_iota(jnp.int32, (rows, columns), 0)
    b = lax.broadcasted_iota(jnp.int32, (rows, columns), 1)
    return (a % patches == b % patches).astype(F32)


def softmax(a, b, mask):
    w = jnp.exp(mm(a.astype(BF16), b.astype(BF16), NT) * HDIM ** (-0.5)) * mask
    return w / jnp.sum(w, axis=-1, keepdims=True)


def kernel(
    C, H, R, G,
    tok, pos, gain1, cot3, qkv, ow, lay_ref, inp_ref,
    hid, cot, gain8, acc, wall, wo, hall, call, gall, normed, inv, proj, gm, wts, aggs, gq2, gsend, grecv,
    grads, s1, r1, s2, r2, own1, own2, corr, rcorr,
    loc, wsnd, wrcv, hs, hr, cs, cr, gs, gr, as_, ar, gas, gar, s1s, s1r, s2s, s2r, ks, kr,
):
    c, h, r = lax.axis_index("chan"), lax.axis_index("head"), lax.axis_index("region")
    T, W = hid.shape
    patches = tok.shape[1]
    S, F = qkv.shape[1], qkv.shape[2]
    FG = F // G
    heads = FG // HDIM
    chg = T // patches
    square = C == 4 and R == 2
    half = S // 2

    def remote(src, dst, ss, rs, **where):
        return pltpu.make_async_remote_copy(
            src_ref=src, dst_ref=dst, send_sem=ss, recv_sem=rs, device_id=where, device_id_type=MESH
        )

    barrier = pltpu.get_barrier_semaphore()
    for k in range(1, C):
        pl.semaphore_signal(barrier, inc=1, device_id={"chan": lax.rem(c + k, C)}, device_id_type=MESH)
    for k in range(1, H):
        pl.semaphore_signal(barrier, inc=1, device_id={"head": lax.rem(h + k, H)}, device_id_type=MESH)
    extra = 0
    if square:
        extra = 1
        pl.semaphore_signal(barrier, inc=1, device_id={"region": 1 - r}, device_id_type=MESH)

    own_w = []
    for n in range(G):
        dst = wall.at[n, :, pl.ds(pl.multiple_of(c * S, S), S)]
        cp = pltpu.make_async_copy(qkv.at[:, :, pl.ds(n * FG, FG)], dst, loc.at[H + n])
        cp.start()
        own_w.append(cp)
    own_o = []
    for i in range(H):
        cp = pltpu.make_async_copy(ow.at[:, pl.ds(i * W, W)], wo.at[i], loc.at[i])
        cp.start()
        own_o.append(cp)
    pl.semaphore_wait(barrier, C - 1 + H - 1 + extra)

    sent = []

    def to_heads(src, buf, ss, rs):
        for k in range(1, H):
            cp = remote(src, buf.at[h], ss.at[k - 1], rs.at[k - 1], head=lax.rem(h + k, H))
            cp.start()
            sent.append(cp)

    def from_heads(buf, ss, rs):
        for k in range(1, H):
            slot = buf.at[lax.rem(h + H - k, H)]
            remote(slot, slot, ss.at[k - 1], rs.at[k - 1], head=lax.rem(h + k, H)).wait_recv()

    def rows_of(n, block, part):
        return wall.at[n, :, pl.ds(pl.multiple_of(block * S + part * half, half), half)]

    if square:
        y, x = c // 2, c % 2
        xn, yn, dg = y * 2 + 1 - x, (1 - y) * 2 + x, (1 - y) * 2 + 1 - x
        near = (xn * (1 - r) + yn * r, yn * (1 - r) + xn * r)
        mate_near = (near[1], near[0])
        blocks = (near[0], near[1], dg)
        mate_blocks = (mate_near[0], mate_near[1], dg)

        def put(slot, j, src, block, part, **where):
            i = slot * G + j
            cp = remote(src, rows_of(j, block, part), wsnd.at[i], wrcv.at[i], **where)
            cp.start()
            sent.append(cp)

        def took(slot, j):
            i = slot * G + j
            if slot < 3:
                ref = rows_of(j, blocks[slot], r)
            else:
                ref = rows_of(j, mate_blocks[slot - 3], 1 - r)
            remote(ref, ref, wsnd.at[i], wrcv.at[i], region=1 - r).wait_recv()

        def pass_on(slot, j):
            took(slot, j)
            src = rows_of(j, blocks[slot], r)
            if slot == 0:
                put(2, j, src, blocks[0], r, chan=near[1])
            put(3 + slot, j, src, blocks[slot], r, region=1 - r)

    if square:
        for n in range(G):
            src = qkv.at[:, pl.ds(pl.multiple_of(r * half, half), half), pl.ds(n * FG, FG)]
            put(0, n, src, c, r, chan=near[0])
            put(1, n, src, c, r, chan=near[1])
    else:
        for n in range(G):
            for k in range(1, C):
                i = n * (C - 1) + k - 1
                src = qkv.at[:, :, pl.ds(n * FG, FG)]
                dst = wall.at[n, :, pl.ds(pl.multiple_of(c * S, S), S)]
                cp = remote(src, dst, wsnd.at[i], wrcv.at[i], chan=lax.rem(c + k, C))
                cp.start()
                sent.append(cp)
    hidden = (tok[...].astype(F32) + pos[...].astype(F32)[:, None, :]).astype(BF16)
    hid[...] = hidden.reshape(T, W)
    gain8[...] = jnp.broadcast_to(gain1[...].astype(F32), gain8.shape)
    to_heads(hid, hall, hs, hr)
    to_heads(gain8, gall, gs, gr)
    cot[...] = cot3[...].reshape(T, W)
    to_heads(cot, call, cs, cr)
    hall[h] = hid[...]
    call[h] = cot[...]
    gall[h] = gain8[...]

    if square:
        pass_on(0, 0)
        pass_on(1, 0)

    from_heads(hall, hs, hr)
    from_heads(gall, gs, gr)
    total = jnp.zeros((T, 1), F32)
    for i in range(H):
        b = hall[i].astype(F32)
        total += jnp.sum(b * b, axis=-1, keepdims=True)
    scale = lax.rsqrt(total / (H * W) + 1e-05)
    inv[...] = jnp.broadcast_to(scale, inv.shape)

    def norm_block(i, carry):
        normed[i] = (hall[i].astype(F32) * inv[:, :1] * gall[i][:1, :]).astype(BF16)
        return carry

    lax.fori_loop(0, H, norm_block, 0)

    def weights(n):
        own_w[n].wait()
        if square:
            pass_on(2, n)
            for slot in (3, 4, 5):
                took(slot, n)
        else:
            for k in range(1, C):
                ref = wall.at[n, :, pl.ds(pl.multiple_of(lax.rem(c + C - k, C) * S, S), S)]
                i = n * (C - 1) + k - 1
                remote(ref, ref, wsnd.at[i], wrcv.at[i], chan=lax.rem(c + k, C)).wait_recv()

    def to_groups(n, src_of, buf, ss, rs):
        for k in range(1, C):
            peer = lax.rem(c + k, C)
            i = n * (C - 1) + k - 1
            cp = remote(src_of(peer), buf.at[n, c], ss.at[i], rs.at[i], chan=peer)
            cp.start()
            sent.append(cp)

    def from_groups(n, buf, ss, rs):
        for k in range(1, C):
            slot = buf.at[n, lax.rem(c + C - k, C)]
            i = n * (C - 1) + k - 1
            remote(slot, slot, ss.at[i], rs.at[i], chan=lax.rem(c + k, C)).wait_recv()

    mask = same_patch(T, T, patches)
    mask2 = same_patch(T, C * patches, patches)

    def forward(n):
        own1[:, : 3 * FG] = jnp.zeros((T, 3 * FG), F32)

        def project(i, carry):
            rows = pl.ds(pl.multiple_of(i * W, W), W)
            for j in range(3):
                own1[:, j * FG : (j + 1) * FG] += mm(normed[i], wall[n, j, rows, :], NN)
            return carry

        lax.fori_loop(0, H, project, 0)
        for j in range(3):
            proj[n, j] = own1[:, j * FG : (j + 1) * FG].astype(BF16)
        for e in range(heads):
            cols = slice(e * HDIM, (e + 1) * HDIM)
            whole = slice(n * FG + e * HDIM, n * FG + (e + 1) * HDIM)
            qn, _ = unit(proj[n, 0][:, cols].astype(F32))
            kn, _ = unit(proj[n, 1][:, cols].astype(F32))
            w = softmax(qn, kn, mask)
            wts[n, e] = w
            first = mm(w.astype(BF16), proj[n, 2][:, cols], NN)
            own2[:, whole] = first
            mean = jnp.mean(first.reshape(chg, patches, HDIM), axis=0)
            own1[:patches, cols] = mean.astype(BF16).astype(F32)
        aggs[n, c] = own1[:patches, :FG]
        to_groups(n, lambda peer: aggs.at[n, c], aggs, as_, ar)

    def across(n):
        from_groups(n, aggs, as_, ar)
        for e in range(heads):
            cols = slice(e * HDIM, (e + 1) * HDIM)
            whole = slice(n * FG + e * HDIM, n * FG + (e + 1) * HDIM)
            a = aggs[n][:, :, cols].reshape(C * patches, HDIM)
            a16 = a.astype(BF16)
            qn, rq = unit(proj[n, 0][:, cols].astype(F32))
            an, ra = unit(a)
            w = softmax(qn, an, mask2)
            w16 = w.astype(BF16)
            own2[:, whole] += mm(w16, a16, NN)
            g16 = gm[:, whole].astype(BF16)
            dw = mm(g16, a16, NT)
            ds = w * (dw - jnp.sum(w * dw, axis=-1, keepdims=True)) * HDIM ** (-0.5)
            ds16 = ds.astype(BF16)
            gq2[:, whole] = unit_back(qn, rq, mm(ds16, an.astype(BF16), NN))
            da = mm(w16, g16, TN) + unit_back(an, ra, mm(ds16, qn.astype(BF16), TN))
            gsend[n, :, :, cols] = da.reshape(C, patches, HDIM)
        to_groups(n, lambda peer: gsend.at[n, peer], grecv, gas, gar)
        grecv[n, c] = gsend[n, c]

    def within(n):
        from_groups(n, grecv, gas, gar)
        back = grecv[n, 0]
        for i in range(1, C):
            back = back + grecv[n, i]
        back = back / chg
        for e in range(heads):
            cols = slice(e * HDIM, (e + 1) * HDIM)
            whole = slice(n * FG + e * HDIM, n * FG + (e + 1) * HDIM)
            lift = jnp.broadcast_to(back[None, :, cols], (chg, patches, HDIM)).reshape(T, HDIM)
            g16 = (gm[:, whole] + lift).astype(BF16)
            qn, rq = unit(proj[n, 0][:, cols].astype(F32))
            kn, rk = unit(proj[n, 1][:, cols].astype(F32))
            w = wts[n, e]
            dw = mm(g16, proj[n, 2][:, cols], NT)
            ds = w * (dw - jnp.sum(w * dw, axis=-1, keepdims=True)) * HDIM ** (-0.5)
            ds16 = ds.astype(BF16)
            dq = unit_back(qn, rq, mm(ds16, kn.astype(BF16), NN)) + gq2[:, whole]
            dk = unit_back(kn, rk, mm(ds16, qn.astype(BF16), TN))
            grads[0, :, cols] = dq.astype(BF16)
            grads[1, :, cols] = dk.astype(BF16)
            grads[2, :, cols] = mm(w.astype(BF16), g16, TN).astype(BF16)

    def back_proj(n, block):
        rows = pl.ds(pl.multiple_of(block * W, W), W)
        total = mm(grads[0], wall[n, 0, rows, :], NT)
        total += mm(grads[1], wall[n, 1, rows, :], NT)
        return total + mm(grads[2], wall[n, 2, rows, :], NT)

    if square:
        for n in range(1, G):
            pass_on(0, n)
            pass_on(1, n)
    for n in range(G):
        weights(n)
        forward(n)
        if n == 0:
            for cp in own_o:
                cp.wait()
            from_heads(call, cs, cr)
            gm[...] = jnp.zeros_like(gm)

            def mixed_block(i, carry):
                gm[...] += mm(call[i], wo[i], NT)
                return carry

            lax.fori_loop(0, H, mixed_block, 0)
        across(n)
        if n < G - 1:
            within(n)

            def add_block(i, carry):
                part = back_proj(n, i)
                acc[i] = part if n == 0 else acc[i] + part
                return carry

            lax.fori_loop(0, H, add_block, 0)

    mixed = own2[:, :F].astype(BF16)
    for k in range(1, H):
        peer = lax.rem(h + k, H)
        s1[k - 1] = mm(mixed, wo[peer], NN).astype(BF16)
        cp = remote(s1.at[k - 1], r1.at[k - 1], s1s.at[k - 1], s1r.at[k - 1], head=peer)
        cp.start()
        sent.append(cp)
    own1[...] = mm(mixed, wo[h], NN)

    within(G - 1)

    dots = jnp.zeros((T, 1), F32)
    for k in list(range(1, H)) + [0]:
        peer = lax.rem(h + k, H)
        part = back_proj(G - 1, peer)
        own2[...] = part if G == 1 else acc[peer] + part
        if k:
            s2[k - 1] = own2[...].astype(BF16)
            cp = remote(s2.at[k - 1], r2.at[k - 1], s2s.at[k - 1], s2r.at[k - 1], head=peer)
            cp.start()
            sent.append(cp)
        dots += jnp.sum(hall[peer].astype(F32) * gall[peer][:1, :] * own2[...], axis=-1, keepdims=True)
    corr[...] = jnp.broadcast_to(dots, corr.shape)
    for k in range(1, H):
        cp = remote(corr, rcorr.at[k - 1], ks.at[k - 1], kr.at[k - 1], head=lax.rem(h + k, H))
        cp.start()
        sent.append(cp)

    def from_shares(buf, ss, rs, k):
        slot = buf.at[k - 1]
        remote(slot, slot, ss.at[k - 1], rs.at[k - 1], head=lax.rem(h + k, H)).wait_recv()

    for k in range(1, H):
        from_shares(r1, s1s, s1r, k)
        own1[...] += r1[k - 1].astype(F32)
    lay_ref[...] = (hid[...].astype(F32) + own1[...]).astype(BF16).reshape(lay_ref.shape)
    for k in range(1, H):
        from_shares(r2, s2s, s2r, k)
        own2[...] += r2[k - 1].astype(F32)
    for k in range(1, H):
        from_shares(rcorr, ks, kr, k)
        corr_k = rcorr[k - 1]
        dots += corr_k[:, :1]
    ir = inv[:, :1]
    grad = ir * gain8[:1, :] * own2[...] - hid[...].astype(F32) * (ir * ir * ir * dots / (H * W))
    inp_ref[...] = (cot[...].astype(F32) + grad).astype(BF16).reshape(inp_ref.shape)
    for cp in sent:
        cp.wait_send()


def per_device(C, H, R, tokens, position, gain, qkv_weight, out_weight, cotangent):
    channels, patches, W = tokens.shape
    T = channels * patches
    S, F = qkv_weight.shape[1:]
    G = 2 if F % (4 * HDIM) == 0 else 1
    FG = F // G
    heads = FG // HDIM
    D = S * C
    V = pltpu.VMEM
    dma = lambda n: pltpu.SemaphoreType.DMA((n,))
    nw = 6 * G if (C == 4 and R == 2) else G * (C - 1)
    z, g = H - 1, G * (C - 1)
    vm = pl.BlockSpec(memory_space=pltpu.VMEM)
    hbm = pl.BlockSpec(memory_space=pl.ANY)
    return pl.pallas_call(
        functools.partial(kernel, C, H, R, G),
        out_shape=[jax.ShapeDtypeStruct(tokens.shape, BF16)] * 2,
        in_specs=[vm, vm, vm, vm, hbm, hbm],
        out_specs=[vm, vm],
        scratch_shapes=[
            V((T, W), BF16), V((T, W), BF16), V((8, W), F32), V((H, T, W), F32),
            V((G, 3, D, FG), BF16), V((H, F, W), BF16), V((H, T, W), BF16), V((H, T, W), BF16),
            V((H, 8, W), F32), V((H, T, W), BF16), V((T, HDIM), F32), V((G, 3, T, FG), BF16),
            V((T, F), F32), V((G, heads, T, T), F32), V((G, C, patches, FG), F32), V((T, F), F32),
            V((G, C, patches, FG), F32), V((G, C, patches, FG), F32), V((3, T, FG), BF16),
            V((z, T, W), BF16), V((z, T, W), BF16), V((z, T, W), BF16), V((z, T, W), BF16),
            V((T, W), F32), V((T, W), F32), V((T, HDIM), F32), V((z, T, HDIM), F32),
            dma(G + H), dma(nw), dma(nw), dma(z), dma(z), dma(z), dma(z), dma(z), dma(z),
            dma(g), dma(g), dma(g), dma(g), dma(z), dma(z), dma(z), dma(z), dma(z), dma(z),
        ],
        compiler_params=pltpu.CompilerParams(
            collective_id=0, has_side_effects=True, vmem_limit_bytes=50 * 1024 * 1024
        ),
    )(tokens, position, gain[None, :], cotangent, qkv_weight, out_weight)


def solution(mesh):
    C, H, R = (mesh.shape[a] for a in ("chan", "head", "region"))
    return jax.shard_map(
        functools.partial(per_device, C, H, R),
        mesh=mesh,
        in_specs=(
            P("chan", "region", "head"),
            P("chan", "head"),
            P("head"),
            P(None, "chan", "head"),
            P("head", None),
            P("chan", "region", "head"),
        ),
        out_specs=(P("chan", "region", "head"), P("chan", "region", "head")),
        check_vma=False,
    )
```

```python
import functools

import jax
import jax.numpy as jnp
from jax import lax
from jax.experimental import pallas as pl
from jax.experimental.pallas import tpu as pltpu
from jax.sharding import PartitionSpec as P

HDIM = 128
MESH = pl.DeviceIdType.MESH
F32 = jnp.float32
BF16 = jnp.bfloat16

NN = (((1,), (0,)), ((), ()))
NT = (((1,), (1,)), ((), ()))
TN = (((0,), (0,)), ((), ()))


def mm(a, b, dims):
    return lax.dot_general(a, b, dims, preferred_element_type=F32)


def unit(u):
    r = lax.rsqrt(jnp.mean(u * u, axis=-1, keepdims=True) + 1e-06)
    return u * r, r


def unit_back(y, r, dy):
    return r * (dy - y * jnp.mean(y * dy, axis=-1, keepdims=True))


def same_patch(rows, columns, patches):
    a = lax.broadcasted_iota(jnp.int32, (rows, columns), 0)
    b = lax.broadcasted_iota(jnp.int32, (rows, columns), 1)
    return (a % patches == b % patches).astype(F32)


def softmax(a, b, mask):
    w = jnp.exp(mm(a.astype(BF16), b.astype(BF16), NT) * HDIM ** (-0.5)) * mask
    return w / jnp.sum(w, axis=-1, keepdims=True)


def kernel(
    C, H, R, G,
    tok, pos, gain1, cot3, qkv, ow, lay_ref, inp_ref,
    hid, cot, gain8, acc, acc2, wall, wo, hall, call, gall, normed, inv, proj, gm, wts, aggs, gq2, gsend, grecv,
    grads, s1, r1, s2, r2, own1, own2, corr, rcorr,
    loc, wsnd, wrcv, hs, hr, cs, cr, gs, gr, as_, ar, gas, gar, s1s, s1r, s2s, s2r, ks, kr,
):
    c, h, r = lax.axis_index("chan"), lax.axis_index("head"), lax.axis_index("region")
    T, W = hid.shape
    patches = tok.shape[1]
    S, F = qkv.shape[1], qkv.shape[2]
    FG = F // G
    heads = FG // HDIM
    chg = T // patches
    square = C == 4 and R == 2
    half = S // 2

    def remote(src, dst, ss, rs, **where):
        return pltpu.make_async_remote_copy(
            src_ref=src, dst_ref=dst, send_sem=ss, recv_sem=rs, device_id=where, device_id_type=MESH
        )

    barrier = pltpu.get_barrier_semaphore()
    for k in range(1, C):
        pl.semaphore_signal(barrier, inc=1, device_id={"chan": lax.rem(c + k, C)}, device_id_type=MESH)
    for k in range(1, H):
        pl.semaphore_signal(barrier, inc=1, device_id={"head": lax.rem(h + k, H)}, device_id_type=MESH)
    extra = 0
    if square:
        extra = 1
        pl.semaphore_signal(barrier, inc=1, device_id={"region": 1 - r}, device_id_type=MESH)

    own_w = []
    for n in range(G):
        dst = wall.at[n, :, pl.ds(pl.multiple_of(c * S, S), S)]
        cp = pltpu.make_async_copy(qkv.at[:, :, pl.ds(n * FG, FG)], dst, loc.at[H + n])
        cp.start()
        own_w.append(cp)
    own_o = []
    for i in range(H):
        cp = pltpu.make_async_copy(ow.at[:, pl.ds(i * W, W)], wo.at[i], loc.at[i])
        cp.start()
        own_o.append(cp)
    pl.semaphore_wait(barrier, C - 1 + H - 1 + extra)

    sent = []

    def to_heads(src, buf, ss, rs):
        for k in range(1, H):
            cp = remote(src, buf.at[h], ss.at[k - 1], rs.at[k - 1], head=lax.rem(h + k, H))
            cp.start()
            sent.append(cp)

    def from_heads(buf, ss, rs):
        for k in range(1, H):
            slot = buf.at[lax.rem(h + H - k, H)]
            remote(slot, slot, ss.at[k - 1], rs.at[k - 1], head=lax.rem(h + k, H)).wait_recv()

    def rows_of(j, block, part):
        return wall.at[0, j, pl.ds(pl.multiple_of(block * S + part * half, half), half)]

    if square:
        y, x = c // 2, c % 2
        xn, yn, dg = y * 2 + 1 - x, (1 - y) * 2 + x, (1 - y) * 2 + 1 - x
        near = (xn * (1 - r) + yn * r, yn * (1 - r) + xn * r)
        mate_near = (near[1], near[0])
        blocks = (near[0], near[1], dg)
        mate_blocks = (mate_near[0], mate_near[1], dg)

        def put(slot, j, src, block, part, **where):
            i = slot * 3 + j
            cp = remote(src, rows_of(j, block, part), wsnd.at[i], wrcv.at[i], **where)
            cp.start()
            sent.append(cp)

        def took(slot, j):
            i = slot * 3 + j
            if slot < 3:
                ref = rows_of(j, blocks[slot], r)
            else:
                ref = rows_of(j, mate_blocks[slot - 3], 1 - r)
            remote(ref, ref, wsnd.at[i], wrcv.at[i], region=1 - r).wait_recv()

        def pass_on(slot, j):
            took(slot, j)
            src = rows_of(j, blocks[slot], r)
            if slot == 0:
                put(2, j, src, blocks[0], r, chan=near[1])
            put(3 + slot, j, src, blocks[slot], r, region=1 - r)

    if square:
        for j in range(3):
            src = qkv.at[j, pl.ds(pl.multiple_of(r * half, half), half)]
            put(0, j, src, c, r, chan=near[0])
            put(1, j, src, c, r, chan=near[1])
    else:
        for n in range(G):
            for k in range(1, C):
                i = n * (C - 1) + k - 1
                src = qkv.at[:, :, pl.ds(n * FG, FG)]
                dst = wall.at[n, :, pl.ds(pl.multiple_of(c * S, S), S)]
                cp = remote(src, dst, wsnd.at[i], wrcv.at[i], chan=lax.rem(c + k, C))
                cp.start()
                sent.append(cp)
    hidden = (tok[...].astype(F32) + pos[...].astype(F32)[:, None, :]).astype(BF16)
    hid[...] = hidden.reshape(T, W)
    gain8[...] = jnp.broadcast_to(gain1[...].astype(F32), gain8.shape)
    to_heads(hid, hall, hs, hr)
    to_heads(gain8, gall, gs, gr)
    cot[...] = cot3[...].reshape(T, W)
    to_heads(cot, call, cs, cr)
    hall[h] = hid[...]
    call[h] = cot[...]
    gall[h] = gain8[...]

    if square:
        pass_on(0, 0)
        pass_on(1, 0)

    from_heads(hall, hs, hr)
    from_heads(gall, gs, gr)
    total = jnp.zeros((T, 1), F32)
    for i in range(H):
        b = hall[i].astype(F32)
        total += jnp.sum(b * b, axis=-1, keepdims=True)
    scale = lax.rsqrt(total / (H * W) + 1e-05)
    inv[...] = jnp.broadcast_to(scale, inv.shape)

    def norm_block(i, carry):
        normed[i] = (hall[i].astype(F32) * inv[:, :1] * gall[i][:1, :]).astype(BF16)
        return carry

    lax.fori_loop(0, H, norm_block, 0)

    def weights(n):
        own_w[n].wait()
        if square:
            for j in range(3):
                pass_on(2, j)
        else:
            for k in range(1, C):
                ref = wall.at[n, :, pl.ds(pl.multiple_of(lax.rem(c + C - k, C) * S, S), S)]
                i = n * (C - 1) + k - 1
                remote(ref, ref, wsnd.at[i], wrcv.at[i], chan=lax.rem(c + k, C)).wait_recv()

    def to_groups(n, src_of, buf, ss, rs):
        for k in range(1, C):
            peer = lax.rem(c + k, C)
            i = n * (C - 1) + k - 1
            cp = remote(src_of(peer), buf.at[n, c], ss.at[i], rs.at[i], chan=peer)
            cp.start()
            sent.append(cp)

    def from_groups(n, buf, ss, rs):
        for k in range(1, C):
            slot = buf.at[n, lax.rem(c + C - k, C)]
            i = n * (C - 1) + k - 1
            remote(slot, slot, ss.at[i], rs.at[i], chan=lax.rem(c + k, C)).wait_recv()

    mask = same_patch(T, T, patches)
    mask2 = same_patch(T, C * patches, patches)

    def forward(n):
        for j in range(3):
            if square:
                for slot in (3, 4, 5):
                    took(slot, j)
            own1[:, :FG] = jnp.zeros((T, FG), F32)

            def project(i, carry):
                rows = pl.ds(pl.multiple_of(i * W, W), W)
                own1[:, :FG] += mm(normed[i], wall[n, j, rows, :], NN)
                return carry

            lax.fori_loop(0, H, project, 0)
            proj[n, j] = own1[:, :FG].astype(BF16)
        for e in range(heads):
            cols = slice(e * HDIM, (e + 1) * HDIM)
            whole = slice(n * FG + e * HDIM, n * FG + (e + 1) * HDIM)
            qn, _ = unit(proj[n, 0][:, cols].astype(F32))
            kn, _ = unit(proj[n, 1][:, cols].astype(F32))
            w = softmax(qn, kn, mask)
            wts[n, e] = w
            first = mm(w.astype(BF16), proj[n, 2][:, cols], NN)
            own2[:, whole] = first
            mean = jnp.mean(first.reshape(chg, patches, HDIM), axis=0)
            own1[:patches, cols] = mean.astype(BF16).astype(F32)
        aggs[n, c] = own1[:patches, :FG]
        to_groups(n, lambda peer: aggs.at[n, c], aggs, as_, ar)

    def across(n):
        from_groups(n, aggs, as_, ar)
        for e in range(heads):
            cols = slice(e * HDIM, (e + 1) * HDIM)
            whole = slice(n * FG + e * HDIM, n * FG + (e + 1) * HDIM)
            a = aggs[n][:, :, cols].reshape(C * patches, HDIM)
            a16 = a.astype(BF16)
            qn, rq = unit(proj[n, 0][:, cols].astype(F32))
            an, ra = unit(a)
            w = softmax(qn, an, mask2)
            w16 = w.astype(BF16)
            own2[:, whole] += mm(w16, a16, NN)
            g16 = gm[:, whole].astype(BF16)
            dw = mm(g16, a16, NT)
            ds = w * (dw - jnp.sum(w * dw, axis=-1, keepdims=True)) * HDIM ** (-0.5)
            ds16 = ds.astype(BF16)
            gq2[:, whole] = unit_back(qn, rq, mm(ds16, an.astype(BF16), NN))
            da = mm(w16, g16, TN) + unit_back(an, ra, mm(ds16, qn.astype(BF16), TN))
            gsend[n, :, :, cols] = da.reshape(C, patches, HDIM)
        to_groups(n, lambda peer: gsend.at[n, peer], grecv, gas, gar)
        grecv[n, c] = gsend[n, c]

    def within(n):
        from_groups(n, grecv, gas, gar)
        back = grecv[n, 0]
        for i in range(1, C):
            back = back + grecv[n, i]
        back = back / chg
        for e in range(heads):
            cols = slice(e * HDIM, (e + 1) * HDIM)
            whole = slice(n * FG + e * HDIM, n * FG + (e + 1) * HDIM)
            lift = jnp.broadcast_to(back[None, :, cols], (chg, patches, HDIM)).reshape(T, HDIM)
            g16 = (gm[:, whole] + lift).astype(BF16)
            qn, rq = unit(proj[n, 0][:, cols].astype(F32))
            kn, rk = unit(proj[n, 1][:, cols].astype(F32))
            w = wts[n, e]
            dw = mm(g16, proj[n, 2][:, cols], NT)
            ds = w * (dw - jnp.sum(w * dw, axis=-1, keepdims=True)) * HDIM ** (-0.5)
            ds16 = ds.astype(BF16)
            dq = unit_back(qn, rq, mm(ds16, kn.astype(BF16), NN)) + gq2[:, whole]
            dk = unit_back(kn, rk, mm(ds16, qn.astype(BF16), TN))
            grads[0, :, cols] = dq.astype(BF16)
            grads[1, :, cols] = dk.astype(BF16)
            grads[2, :, cols] = mm(w.astype(BF16), g16, TN).astype(BF16)

    def back_proj(n, block):
        rows = pl.ds(pl.multiple_of(block * W, W), W)
        total = mm(grads[0], wall[n, 0, rows, :], NT)
        total += mm(grads[1], wall[n, 1, rows, :], NT)
        return total + mm(grads[2], wall[n, 2, rows, :], NT)

    if square:
        pass_on(0, 1)
        pass_on(1, 1)
    for cp in own_o:
        cp.wait()
    from_heads(call, cs, cr)
    gm[...] = jnp.zeros_like(gm)

    def mixed_block(i, carry):
        gm[...] += mm(call[i], wo[i], NT)
        return carry

    if square:
        pass_on(0, 2)
        pass_on(1, 2)
    lax.fori_loop(0, H, mixed_block, 0)
    weights(0)
    forward(0)
    across(0)

    later = []

    def chain_copy(way, m, snd, rcv, ss, rs):
        i = way * (H - 1) + m
        peer = lax.rem(h + 1, H) if way == 0 else lax.rem(h + H - 1, H)
        return remote(snd.at[i], rcv.at[i], ss.at[i], rs.at[i], head=peer)

    def chain_step(m, share, snd, rcv, ss, rs):
        for way in range(2):
            d = H - 1 - m if way == 0 else m
            first = (h == 0) if way == 0 else (h == H - 1)
            sends = (h < d) if way == 0 else (h > d)
            i = way * (H - 1) + m
            cp = chain_copy(way, m, snd, rcv, ss, rs)

            @pl.when(jnp.logical_and(sends, jnp.logical_not(first)))
            def _():
                cp.wait_recv()
                snd[i] = (share[d] + rcv[i].astype(F32)).astype(BF16)
                cp.start()

            later.append((sends, cp))

    def chain_open(d, share, snd, rcv, ss, rs):
        for way in range(2):
            m = H - 1 - d if way == 0 else d
            if m > H - 2:
                continue
            i = way * (H - 1) + m
            first = (h == 0) if way == 0 else (h == H - 1)

            @pl.when(first)
            def _():
                snd[i] = share[d].astype(BF16)
                chain_copy(way, m, snd, rcv, ss, rs).start()

    def chain_end(share, snd, rcv, ss, rs, total):
        total[...] = share[h]
        for way in range(2):
            for m in range(H - 1):
                d = H - 1 - m if way == 0 else m
                i = way * (H - 1) + m

                @pl.when(h == d)
                def _():
                    chain_copy(way, m, snd, rcv, ss, rs).wait_recv()
                    total[...] += rcv[i].astype(F32)

    order = []
    for m in range((H + 1) // 2):
        order += [H - 1 - m] + ([m] if m != H - 1 - m else [])
    mixed = own2[:, :F].astype(BF16)
    one = (acc, s1, r1, s1s, s1r)
    two = (acc2, s2, r2, s2s, s2r)
    for d in order:
        acc[d] = mm(mixed, wo[d], NN)
        chain_open(d, *one)
    chain_step(0, *one)
    within(0)
    for m in range(1, H - 2):
        chain_step(m, *one)

    dots = jnp.zeros((T, 1), F32)
    for d in order:
        part = back_proj(0, d)
        acc2[d] = part
        chain_open(d, *two)
        dots += jnp.sum(hall[d].astype(F32) * gall[d][:1, :] * part, axis=-1, keepdims=True)
    for m in range(max(1, H - 2), H - 1):
        chain_step(m, *one)
    corr[...] = jnp.broadcast_to(dots, corr.shape)
    for k in range(1, H):
        cp = remote(corr, rcorr.at[k - 1], ks.at[k - 1], kr.at[k - 1], head=lax.rem(h + k, H))
        cp.start()
        sent.append(cp)
    for m in range(H - 1):
        chain_step(m, *two)
    chain_end(*one, own1)
    lay_ref[...] = (hid[...].astype(F32) + own1[...]).astype(BF16).reshape(lay_ref.shape)
    for k in range(1, H):
        remote(rcorr.at[k - 1], rcorr.at[k - 1], ks.at[k - 1], kr.at[k - 1], head=lax.rem(h + k, H)).wait_recv()
        corr_k = rcorr[k - 1]
        dots += corr_k[:, :1]
    chain_end(*two, own2)
    ir = inv[:, :1]
    grad = ir * gain8[:1, :] * own2[...] - hid[...].astype(F32) * (ir * ir * ir * dots / (H * W))
    inp_ref[...] = (cot[...].astype(F32) + grad).astype(BF16).reshape(inp_ref.shape)
    for cp in sent:
        cp.wait_send()
    for sends, cp in later:
        pl.when(sends)(cp.wait_send)


def per_device(C, H, R, tokens, position, gain, qkv_weight, out_weight, cotangent):
    channels, patches, W = tokens.shape
    T = channels * patches
    S, F = qkv_weight.shape[1:]
    G = 1
    FG = F // G
    heads = FG // HDIM
    D = S * C
    V = pltpu.VMEM
    dma = lambda n: pltpu.SemaphoreType.DMA((n,))
    nw = 18 if (C == 4 and R == 2) else G * (C - 1)
    z, g = H - 1, G * (C - 1)
    vm = pl.BlockSpec(memory_space=pltpu.VMEM)
    hbm = pl.BlockSpec(memory_space=pl.ANY)
    return pl.pallas_call(
        functools.partial(kernel, C, H, R, G),
        out_shape=[jax.ShapeDtypeStruct(tokens.shape, BF16)] * 2,
        in_specs=[vm, vm, vm, vm, hbm, hbm],
        out_specs=[vm, vm],
        scratch_shapes=[
            V((T, W), BF16), V((T, W), BF16), V((8, W), F32), V((H, T, W), F32), V((H, T, W), F32),
            V((G, 3, D, FG), BF16), V((H, F, W), BF16), V((H, T, W), BF16), V((H, T, W), BF16),
            V((H, 8, W), F32), V((H, T, W), BF16), V((T, HDIM), F32), V((G, 3, T, FG), BF16),
            V((T, F), F32), V((G, heads, T, T), F32), V((G, C, patches, FG), F32), V((T, F), F32),
            V((G, C, patches, FG), F32), V((G, C, patches, FG), F32), V((3, T, FG), BF16),
            V((2 * z, T, W), BF16), V((2 * z, T, W), BF16), V((2 * z, T, W), BF16), V((2 * z, T, W), BF16),
            V((T, W), F32), V((T, W), F32), V((T, HDIM), F32), V((z, T, HDIM), F32),
            dma(G + H), dma(nw), dma(nw), dma(z), dma(z), dma(z), dma(z), dma(z), dma(z),
            dma(g), dma(g), dma(g), dma(g), dma(2 * z), dma(2 * z), dma(2 * z), dma(2 * z), dma(z), dma(z),
        ],
        compiler_params=pltpu.CompilerParams(
            collective_id=0, has_side_effects=True, vmem_limit_bytes=50 * 1024 * 1024
        ),
    )(tokens, position, gain[None, :], cotangent, qkv_weight, out_weight)


def solution(mesh):
    C, H, R = (mesh.shape[a] for a in ("chan", "head", "region"))
    return jax.shard_map(
        functools.partial(per_device, C, H, R),
        mesh=mesh,
        in_specs=(
            P("chan", "region", "head"),
            P("chan", "head"),
            P("head"),
            P(None, "chan", "head"),
            P("head", None),
            P("chan", "region", "head"),
        ),
        out_specs=(P("chan", "region", "head"), P("chan", "region", "head")),
        check_vma=False,
    )
```

```python
import functools

import jax
import jax.numpy as jnp
from jax import lax
from jax.experimental import pallas as pl
from jax.experimental.pallas import tpu as pltpu
from jax.sharding import PartitionSpec as P

HDIM = 128
MESH = pl.DeviceIdType.MESH
F32 = jnp.float32
BF16 = jnp.bfloat16

NN = (((1,), (0,)), ((), ()))
NT = (((1,), (1,)), ((), ()))
TN = (((0,), (0,)), ((), ()))


def mm(a, b, dims):
    return lax.dot_general(a, b, dims, preferred_element_type=F32)


def unit(u):
    r = lax.rsqrt(jnp.mean(u * u, axis=-1, keepdims=True) + 1e-06)
    return u * r, r


def unit_back(y, r, dy):
    return r * (dy - y * jnp.mean(y * dy, axis=-1, keepdims=True))


def same_patch(rows, columns, patches):
    a = lax.broadcasted_iota(jnp.int32, (rows, columns), 0)
    b = lax.broadcasted_iota(jnp.int32, (rows, columns), 1)
    return (a % patches == b % patches).astype(F32)


def softmax(a, b, mask):
    w = jnp.exp(mm(a.astype(BF16), b.astype(BF16), NT) * HDIM ** (-0.5)) * mask
    return w / jnp.sum(w, axis=-1, keepdims=True)


def kernel(
    C, H, R, G,
    tok, pos, gain1, cot3, qkv, ow, lay_ref, inp_ref,
    hid, cot, gain8, acc, acc2, wall, wo, hall, call, gall, normed, inv, proj, gm, wts, aggs, gq2, gsend, grecv,
    grads, s1, r1, s2, r2, own1, own2, corr, rcorr,
    loc, wsnd, wrcv, hs, hr, cs, cr, gs, gr, as_, ar, gas, gar, s1s, s1r, s2s, s2r, ks, kr,
):
    c, h, r = lax.axis_index("chan"), lax.axis_index("head"), lax.axis_index("region")
    T, W = hid.shape
    patches = tok.shape[1]
    S, F = qkv.shape[1], qkv.shape[2]
    FG = F // G
    heads = FG // HDIM
    chg = T // patches
    square = C == 4 and R == 2
    half = S // 2

    def remote(src, dst, ss, rs, **where):
        return pltpu.make_async_remote_copy(
            src_ref=src, dst_ref=dst, send_sem=ss, recv_sem=rs, device_id=where, device_id_type=MESH
        )

    barrier = pltpu.get_barrier_semaphore()
    for k in range(1, C):
        pl.semaphore_signal(barrier, inc=1, device_id={"chan": lax.rem(c + k, C)}, device_id_type=MESH)
    for k in range(1, H):
        pl.semaphore_signal(barrier, inc=1, device_id={"head": lax.rem(h + k, H)}, device_id_type=MESH)
    extra = 0
    if square:
        extra = 1
        pl.semaphore_signal(barrier, inc=1, device_id={"region": 1 - r}, device_id_type=MESH)

    own_w = []
    for n in range(G):
        dst = wall.at[n, :, pl.ds(pl.multiple_of(c * S, S), S)]
        cp = pltpu.make_async_copy(qkv.at[:, :, pl.ds(n * FG, FG)], dst, loc.at[H + n])
        cp.start()
        own_w.append(cp)
    own_o = []
    for i in range(H):
        cp = pltpu.make_async_copy(ow.at[:, pl.ds(i * W, W)], wo.at[i], loc.at[i])
        cp.start()
        own_o.append(cp)
    pl.semaphore_wait(barrier, C - 1 + H - 1 + extra)

    sent = []

    def to_heads(src, buf, ss, rs):
        for k in range(1, H):
            cp = remote(src, buf.at[h], ss.at[k - 1], rs.at[k - 1], head=lax.rem(h + k, H))
            cp.start()
            sent.append(cp)

    def from_heads(buf, ss, rs):
        for k in range(1, H):
            slot = buf.at[lax.rem(h + H - k, H)]
            remote(slot, slot, ss.at[k - 1], rs.at[k - 1], head=lax.rem(h + k, H)).wait_recv()

    def rows_of(j, block, part):
        return wall.at[0, j, pl.ds(pl.multiple_of(block * S + part * half, half), half)]

    if square:
        y, x = c // 2, c % 2
        xn, yn, dg = y * 2 + 1 - x, (1 - y) * 2 + x, (1 - y) * 2 + 1 - x
        near = (xn * (1 - r) + yn * r, yn * (1 - r) + xn * r)
        mate_near = (near[1], near[0])
        blocks = (near[0], near[1], dg)
        mate_blocks = (mate_near[0], mate_near[1], dg)

        def put(slot, j, src, block, part, **where):
            i = slot * 3 + j
            cp = remote(src, rows_of(j, block, part), wsnd.at[i], wrcv.at[i], **where)
            cp.start()
            sent.append(cp)

        def took(slot, j):
            i = slot * 3 + j
            if slot < 3:
                ref = rows_of(j, blocks[slot], r)
            else:
                ref = rows_of(j, mate_blocks[slot - 3], 1 - r)
            remote(ref, ref, wsnd.at[i], wrcv.at[i], region=1 - r).wait_recv()

        def pass_on(slot, j):
            took(slot, j)
            src = rows_of(j, blocks[slot], r)
            if slot == 0:
                put(2, j, src, blocks[0], r, chan=near[1])
            put(3 + slot, j, src, blocks[slot], r, region=1 - r)

    if square:
        for j in range(3):
            src = qkv.at[j, pl.ds(pl.multiple_of(r * half, half), half)]
            put(0, j, src, c, r, chan=near[0])
            put(1, j, src, c, r, chan=near[1])
    else:
        for n in range(G):
            for k in range(1, C):
                i = n * (C - 1) + k - 1
                src = qkv.at[:, :, pl.ds(n * FG, FG)]
                dst = wall.at[n, :, pl.ds(pl.multiple_of(c * S, S), S)]
                cp = remote(src, dst, wsnd.at[i], wrcv.at[i], chan=lax.rem(c + k, C))
                cp.start()
                sent.append(cp)
    hidden = (tok[...].astype(F32) + pos[...].astype(F32)[:, None, :]).astype(BF16)
    hid[...] = hidden.reshape(T, W)
    gain8[...] = jnp.broadcast_to(gain1[...].astype(F32), gain8.shape)
    to_heads(hid, hall, hs, hr)
    to_heads(gain8, gall, gs, gr)
    cot[...] = cot3[...].reshape(T, W)
    to_heads(cot, call, cs, cr)
    hall[h] = hid[...]
    call[h] = cot[...]
    gall[h] = gain8[...]

    if square:
        pass_on(0, 0)
        pass_on(1, 0)

    from_heads(hall, hs, hr)
    from_heads(gall, gs, gr)
    total = jnp.zeros((T, 1), F32)
    for i in range(H):
        b = hall[i].astype(F32)
        total += jnp.sum(b * b, axis=-1, keepdims=True)
    scale = lax.rsqrt(total / (H * W) + 1e-05)
    inv[...] = jnp.broadcast_to(scale, inv.shape)

    def norm_block(i, carry):
        normed[i] = (hall[i].astype(F32) * inv[:, :1] * gall[i][:1, :]).astype(BF16)
        return carry

    lax.fori_loop(0, H, norm_block, 0)

    def weights(n):
        own_w[n].wait()
        if not square:
            for k in range(1, C):
                ref = wall.at[n, :, pl.ds(pl.multiple_of(lax.rem(c + C - k, C) * S, S), S)]
                i = n * (C - 1) + k - 1
                remote(ref, ref, wsnd.at[i], wrcv.at[i], chan=lax.rem(c + k, C)).wait_recv()

    def to_groups(n, src_of, buf, ss, rs):
        for k in range(1, C):
            peer = lax.rem(c + k, C)
            i = n * (C - 1) + k - 1
            cp = remote(src_of(peer), buf.at[n, c], ss.at[i], rs.at[i], chan=peer)
            cp.start()
            sent.append(cp)

    def from_groups(n, buf, ss, rs):
        for k in range(1, C):
            slot = buf.at[n, lax.rem(c + C - k, C)]
            i = n * (C - 1) + k - 1
            remote(slot, slot, ss.at[i], rs.at[i], chan=lax.rem(c + k, C)).wait_recv()

    mask = same_patch(T, T, patches)
    mask2 = same_patch(T, C * patches, patches)

    def forward(n):
        for j in range(3):
            if square:
                pass_on(2, j)
                for slot in (3, 4, 5):
                    took(slot, j)
            own1[:, :FG] = jnp.zeros((T, FG), F32)

            def project(i, carry):
                rows = pl.ds(pl.multiple_of(i * W, W), W)
                own1[:, :FG] += mm(normed[i], wall[n, j, rows, :], NN)
                return carry

            lax.fori_loop(0, H, project, 0)
            proj[n, j] = own1[:, :FG].astype(BF16)
        for e in range(heads):
            cols = slice(e * HDIM, (e + 1) * HDIM)
            whole = slice(n * FG + e * HDIM, n * FG + (e + 1) * HDIM)
            qn, _ = unit(proj[n, 0][:, cols].astype(F32))
            kn, _ = unit(proj[n, 1][:, cols].astype(F32))
            w = softmax(qn, kn, mask)
            wts[n, e] = w
            first = mm(w.astype(BF16), proj[n, 2][:, cols], NN)
            own2[:, whole] = first
            mean = jnp.mean(first.reshape(chg, patches, HDIM), axis=0)
            own1[:patches, cols] = mean.astype(BF16).astype(F32)
        aggs[n, c] = own1[:patches, :FG]
        to_groups(n, lambda peer: aggs.at[n, c], aggs, as_, ar)

    def across(n):
        from_groups(n, aggs, as_, ar)
        for e in range(heads):
            cols = slice(e * HDIM, (e + 1) * HDIM)
            whole = slice(n * FG + e * HDIM, n * FG + (e + 1) * HDIM)
            a = aggs[n][:, :, cols].reshape(C * patches, HDIM)
            a16 = a.astype(BF16)
            qn, rq = unit(proj[n, 0][:, cols].astype(F32))
            an, ra = unit(a)
            w = softmax(qn, an, mask2)
            w16 = w.astype(BF16)
            own2[:, whole] += mm(w16, a16, NN)
            g16 = gm[:, whole].astype(BF16)
            dw = mm(g16, a16, NT)
            ds = w * (dw - jnp.sum(w * dw, axis=-1, keepdims=True)) * HDIM ** (-0.5)
            ds16 = ds.astype(BF16)
            gq2[:, whole] = unit_back(qn, rq, mm(ds16, an.astype(BF16), NN))
            da = mm(w16, g16, TN) + unit_back(an, ra, mm(ds16, qn.astype(BF16), TN))
            gsend[n, :, :, cols] = da.reshape(C, patches, HDIM)
        to_groups(n, lambda peer: gsend.at[n, peer], grecv, gas, gar)
        grecv[n, c] = gsend[n, c]

    def within(n):
        from_groups(n, grecv, gas, gar)
        back = grecv[n, 0]
        for i in range(1, C):
            back = back + grecv[n, i]
        back = back / chg
        for e in range(heads):
            cols = slice(e * HDIM, (e + 1) * HDIM)
            whole = slice(n * FG + e * HDIM, n * FG + (e + 1) * HDIM)
            lift = jnp.broadcast_to(back[None, :, cols], (chg, patches, HDIM)).reshape(T, HDIM)
            g16 = (gm[:, whole] + lift).astype(BF16)
            qn, rq = unit(proj[n, 0][:, cols].astype(F32))
            kn, rk = unit(proj[n, 1][:, cols].astype(F32))
            w = wts[n, e]
            dw = mm(g16, proj[n, 2][:, cols], NT)
            ds = w * (dw - jnp.sum(w * dw, axis=-1, keepdims=True)) * HDIM ** (-0.5)
            ds16 = ds.astype(BF16)
            dq = unit_back(qn, rq, mm(ds16, kn.astype(BF16), NN)) + gq2[:, whole]
            dk = unit_back(kn, rk, mm(ds16, qn.astype(BF16), TN))
            grads[0, :, cols] = dq.astype(BF16)
            grads[1, :, cols] = dk.astype(BF16)
            grads[2, :, cols] = mm(w.astype(BF16), g16, TN).astype(BF16)

    def back_proj(n, block):
        rows = pl.ds(pl.multiple_of(block * W, W), W)
        total = mm(grads[0], wall[n, 0, rows, :], NT)
        total += mm(grads[1], wall[n, 1, rows, :], NT)
        return total + mm(grads[2], wall[n, 2, rows, :], NT)

    if square:
        for j in (1, 2):
            pass_on(0, j)
            pass_on(1, j)
    for cp in own_o:
        cp.wait()
    from_heads(call, cs, cr)
    gm[...] = jnp.zeros_like(gm)

    def mixed_block(i, carry):
        gm[...] += mm(call[i], wo[i], NT)
        return carry

    lax.fori_loop(0, H, mixed_block, 0)
    weights(0)
    forward(0)
    across(0)

    later = []

    def chain_copy(way, m, snd, rcv, ss, rs):
        i = way * (H - 1) + m
        peer = lax.rem(h + 1, H) if way == 0 else lax.rem(h + H - 1, H)
        return remote(snd.at[i], rcv.at[i], ss.at[i], rs.at[i], head=peer)

    def chain_step(m, share, snd, rcv, ss, rs):
        for way in range(2):
            d = H - 1 - m if way == 0 else m
            first = (h == 0) if way == 0 else (h == H - 1)
            sends = (h < d) if way == 0 else (h > d)
            i = way * (H - 1) + m
            cp = chain_copy(way, m, snd, rcv, ss, rs)

            @pl.when(jnp.logical_and(sends, jnp.logical_not(first)))
            def _():
                cp.wait_recv()
                snd[i] = (share[d] + rcv[i].astype(F32)).astype(BF16)
                cp.start()

            later.append((sends, cp))

    def chain_open(d, share, snd, rcv, ss, rs):
        for way in range(2):
            m = H - 1 - d if way == 0 else d
            if m > H - 2:
                continue
            i = way * (H - 1) + m
            first = (h == 0) if way == 0 else (h == H - 1)

            @pl.when(first)
            def _():
                snd[i] = share[d].astype(BF16)
                chain_copy(way, m, snd, rcv, ss, rs).start()

    def chain_end(share, snd, rcv, ss, rs, total):
        total[...] = share[h]
        for way in range(2):
            for m in range(H - 1):
                d = H - 1 - m if way == 0 else m
                i = way * (H - 1) + m

                @pl.when(h == d)
                def _():
                    chain_copy(way, m, snd, rcv, ss, rs).wait_recv()
                    total[...] += rcv[i].astype(F32)

    order = []
    for m in range((H + 1) // 2):
        order += [H - 1 - m] + ([m] if m != H - 1 - m else [])
    mixed = own2[:, :F].astype(BF16)
    one = (acc, s1, r1, s1s, s1r)
    two = (acc2, s2, r2, s2s, s2r)
    for d in order:
        acc[d] = mm(mixed, wo[d], NN)
        chain_open(d, *one)
    chain_step(0, *one)
    within(0)
    for m in range(1, H - 2):
        chain_step(m, *one)

    dots = jnp.zeros((T, 1), F32)
    for d in order:
        part = back_proj(0, d)
        acc2[d] = part
        chain_open(d, *two)
        dots += jnp.sum(hall[d].astype(F32) * gall[d][:1, :] * part, axis=-1, keepdims=True)
    for m in range(max(1, H - 2), H - 1):
        chain_step(m, *one)
    corr[...] = jnp.broadcast_to(dots, corr.shape)
    for k in range(1, H):
        cp = remote(corr, rcorr.at[k - 1], ks.at[k - 1], kr.at[k - 1], head=lax.rem(h + k, H))
        cp.start()
        sent.append(cp)
    for m in range(H - 1):
        chain_step(m, *two)
    chain_end(*one, own1)
    lay_ref[...] = (hid[...].astype(F32) + own1[...]).astype(BF16).reshape(lay_ref.shape)
    for k in range(1, H):
        remote(rcorr.at[k - 1], rcorr.at[k - 1], ks.at[k - 1], kr.at[k - 1], head=lax.rem(h + k, H)).wait_recv()
        corr_k = rcorr[k - 1]
        dots += corr_k[:, :1]
    chain_end(*two, own2)
    ir = inv[:, :1]
    grad = ir * gain8[:1, :] * own2[...] - hid[...].astype(F32) * (ir * ir * ir * dots / (H * W))
    inp_ref[...] = (cot[...].astype(F32) + grad).astype(BF16).reshape(inp_ref.shape)
    for cp in sent:
        cp.wait_send()
    for sends, cp in later:
        pl.when(sends)(cp.wait_send)


def per_device(C, H, R, tokens, position, gain, qkv_weight, out_weight, cotangent):
    channels, patches, W = tokens.shape
    T = channels * patches
    S, F = qkv_weight.shape[1:]
    G = 1
    FG = F // G
    heads = FG // HDIM
    D = S * C
    V = pltpu.VMEM
    dma = lambda n: pltpu.SemaphoreType.DMA((n,))
    nw = 18 if (C == 4 and R == 2) else G * (C - 1)
    z, g = H - 1, G * (C - 1)
    vm = pl.BlockSpec(memory_space=pltpu.VMEM)
    hbm = pl.BlockSpec(memory_space=pl.ANY)
    return pl.pallas_call(
        functools.partial(kernel, C, H, R, G),
        out_shape=[jax.ShapeDtypeStruct(tokens.shape, BF16)] * 2,
        in_specs=[vm, vm, vm, vm, hbm, hbm],
        out_specs=[vm, vm],
        scratch_shapes=[
            V((T, W), BF16), V((T, W), BF16), V((8, W), F32), V((H, T, W), F32), V((H, T, W), F32),
            V((G, 3, D, FG), BF16), V((H, F, W), BF16), V((H, T, W), BF16), V((H, T, W), BF16),
            V((H, 8, W), F32), V((H, T, W), BF16), V((T, HDIM), F32), V((G, 3, T, FG), BF16),
            V((T, F), F32), V((G, heads, T, T), F32), V((G, C, patches, FG), F32), V((T, F), F32),
            V((G, C, patches, FG), F32), V((G, C, patches, FG), F32), V((3, T, FG), BF16),
            V((2 * z, T, W), BF16), V((2 * z, T, W), BF16), V((2 * z, T, W), BF16), V((2 * z, T, W), BF16),
            V((T, W), F32), V((T, W), F32), V((T, HDIM), F32), V((z, T, HDIM), F32),
            dma(G + H), dma(nw), dma(nw), dma(z), dma(z), dma(z), dma(z), dma(z), dma(z),
            dma(g), dma(g), dma(g), dma(g), dma(2 * z), dma(2 * z), dma(2 * z), dma(2 * z), dma(z), dma(z),
        ],
        compiler_params=pltpu.CompilerParams(
            collective_id=0, has_side_effects=True, vmem_limit_bytes=50 * 1024 * 1024
        ),
    )(tokens, position, gain[None, :], cotangent, qkv_weight, out_weight)


def solution(mesh):
    C, H, R = (mesh.shape[a] for a in ("chan", "head", "region"))
    return jax.shard_map(
        functools.partial(per_device, C, H, R),
        mesh=mesh,
        in_specs=(
            P("chan", "region", "head"),
            P("chan", "head"),
            P("head"),
            P(None, "chan", "head"),
            P("head", None),
            P("chan", "region", "head"),
        ),
        out_specs=(P("chan", "region", "head"), P("chan", "region", "head")),
        check_vma=False,
    )
```

```python
import functools

import jax
import jax.numpy as jnp
from jax import lax
from jax.experimental import pallas as pl
from jax.experimental.pallas import tpu as pltpu
from jax.sharding import PartitionSpec as P

HDIM = 128
MESH = pl.DeviceIdType.MESH
F32 = jnp.float32
BF16 = jnp.bfloat16

NN = (((1,), (0,)), ((), ()))
NT = (((1,), (1,)), ((), ()))
TN = (((0,), (0,)), ((), ()))


def mm(a, b, dims):
    return lax.dot_general(a, b, dims, preferred_element_type=F32)


def unit(u):
    r = lax.rsqrt(jnp.mean(u * u, axis=-1, keepdims=True) + 1e-06)
    return u * r, r


def unit_back(y, r, dy):
    return r * (dy - y * jnp.mean(y * dy, axis=-1, keepdims=True))


def same_patch(rows, columns, patches):
    a = lax.broadcasted_iota(jnp.int32, (rows, columns), 0)
    b = lax.broadcasted_iota(jnp.int32, (rows, columns), 1)
    return (a % patches == b % patches).astype(F32)


def softmax(a, b, mask):
    w = jnp.exp(mm(a.astype(BF16), b.astype(BF16), NT) * HDIM ** (-0.5)) * mask
    return w / jnp.sum(w, axis=-1, keepdims=True)


def kernel(
    C, H, R, G,
    tok, pos, gain1, cot3, qkv, ow, lay_ref, inp_ref,
    hid, cot, gain8, acc, acc2, wall, wo, hall, call, gall, normed, inv, proj, gm, wts, aggs, gq2, gsend, grecv,
    grads, s1, r1, s2, r2, own1, own2, corr, rcorr,
    loc, wsnd, wrcv, hs, hr, cs, cr, gs, gr, as_, ar, gas, gar, s1s, s1r, s2s, s2r, ks, kr,
):
    c, h, r = lax.axis_index("chan"), lax.axis_index("head"), lax.axis_index("region")
    T, W = hid.shape
    patches = tok.shape[1]
    S, F = qkv.shape[1], qkv.shape[2]
    FG = F // G
    heads = FG // HDIM
    chg = T // patches
    square = C == 4 and R == 2
    half = S // 2

    def remote(src, dst, ss, rs, **where):
        return pltpu.make_async_remote_copy(
            src_ref=src, dst_ref=dst, send_sem=ss, recv_sem=rs, device_id=where, device_id_type=MESH
        )

    barrier = pltpu.get_barrier_semaphore()
    for k in range(1, C):
        pl.semaphore_signal(barrier, inc=1, device_id={"chan": lax.rem(c + k, C)}, device_id_type=MESH)
    for k in range(1, H):
        pl.semaphore_signal(barrier, inc=1, device_id={"head": lax.rem(h + k, H)}, device_id_type=MESH)
    extra = 0
    if square:
        extra = 1
        pl.semaphore_signal(barrier, inc=1, device_id={"region": 1 - r}, device_id_type=MESH)

    own_w = []
    for n in range(G):
        dst = wall.at[n, :, pl.ds(pl.multiple_of(c * S, S), S)]
        cp = pltpu.make_async_copy(qkv.at[:, :, pl.ds(n * FG, FG)], dst, loc.at[H + n])
        cp.start()
        own_w.append(cp)
    own_o = []
    for i in range(H):
        cp = pltpu.make_async_copy(ow.at[:, pl.ds(i * W, W)], wo.at[i], loc.at[i])
        cp.start()
        own_o.append(cp)
    pl.semaphore_wait(barrier, C - 1 + H - 1 + extra)

    sent = []

    def to_heads(src, buf, ss, rs):
        for k in range(1, H):
            cp = remote(src, buf.at[h], ss.at[k - 1], rs.at[k - 1], head=lax.rem(h + k, H))
            cp.start()
            sent.append(cp)

    def from_heads(buf, ss, rs):
        for k in range(1, H):
            slot = buf.at[lax.rem(h + H - k, H)]
            remote(slot, slot, ss.at[k - 1], rs.at[k - 1], head=lax.rem(h + k, H)).wait_recv()

    def rows_of(j, block, part):
        return wall.at[0, j, pl.ds(pl.multiple_of(block * S + part * half, half), half)]

    if square:
        y, x = c // 2, c % 2
        xn, yn, dg = y * 2 + 1 - x, (1 - y) * 2 + x, (1 - y) * 2 + 1 - x
        near = (xn * (1 - r) + yn * r, yn * (1 - r) + xn * r)
        mate_near = (near[1], near[0])
        blocks = (near[0], near[1], dg)
        mate_blocks = (mate_near[0], mate_near[1], dg)

        def put(slot, j, src, block, part, **where):
            i = slot * 3 + j
            cp = remote(src, rows_of(j, block, part), wsnd.at[i], wrcv.at[i], **where)
            cp.start()
            sent.append(cp)

        def took(slot, j):
            i = slot * 3 + j
            if slot < 3:
                ref = rows_of(j, blocks[slot], r)
            else:
                ref = rows_of(j, mate_blocks[slot - 3], 1 - r)
            remote(ref, ref, wsnd.at[i], wrcv.at[i], region=1 - r).wait_recv()

        def pass_on(slot, j):
            took(slot, j)
            src = rows_of(j, blocks[slot], r)
            if slot == 0:
                put(2, j, src, blocks[0], r, chan=near[1])
            put(3 + slot, j, src, blocks[slot], r, region=1 - r)

    if square:
        for j in range(3):
            src = qkv.at[j, pl.ds(pl.multiple_of(r * half, half), half)]
            put(0, j, src, c, r, chan=near[0])
            put(1, j, src, c, r, chan=near[1])
    else:
        for n in range(G):
            for k in range(1, C):
                i = n * (C - 1) + k - 1
                src = qkv.at[:, :, pl.ds(n * FG, FG)]
                dst = wall.at[n, :, pl.ds(pl.multiple_of(c * S, S), S)]
                cp = remote(src, dst, wsnd.at[i], wrcv.at[i], chan=lax.rem(c + k, C))
                cp.start()
                sent.append(cp)
    hidden = (tok[...].astype(F32) + pos[...].astype(F32)[:, None, :]).astype(BF16)
    hid[...] = hidden.reshape(T, W)
    gain8[...] = jnp.broadcast_to(gain1[...].astype(F32), gain8.shape)
    to_heads(hid, hall, hs, hr)
    to_heads(gain8, gall, gs, gr)
    cot[...] = cot3[...].reshape(T, W)
    to_heads(cot, call, cs, cr)
    hall[h] = hid[...]
    call[h] = cot[...]
    gall[h] = gain8[...]

    if square:
        pass_on(0, 0)
        pass_on(1, 0)

    from_heads(hall, hs, hr)
    from_heads(gall, gs, gr)
    total = jnp.zeros((T, 1), F32)
    for i in range(H):
        b = hall[i].astype(F32)
        total += jnp.sum(b * b, axis=-1, keepdims=True)
    scale = lax.rsqrt(total / (H * W) + 1e-05)
    inv[...] = jnp.broadcast_to(scale, inv.shape)

    def norm_block(i, carry):
        normed[i] = (hall[i].astype(F32) * inv[:, :1] * gall[i][:1, :]).astype(BF16)
        return carry

    lax.fori_loop(0, H, norm_block, 0)

    def weights(n):
        own_w[n].wait()
        if square:
            for j in range(3):
                pass_on(2, j)
        else:
            for k in range(1, C):
                ref = wall.at[n, :, pl.ds(pl.multiple_of(lax.rem(c + C - k, C) * S, S), S)]
                i = n * (C - 1) + k - 1
                remote(ref, ref, wsnd.at[i], wrcv.at[i], chan=lax.rem(c + k, C)).wait_recv()

    def to_groups(n, src_of, buf, ss, rs):
        for k in range(1, C):
            peer = lax.rem(c + k, C)
            i = n * (C - 1) + k - 1
            cp = remote(src_of(peer), buf.at[n, c], ss.at[i], rs.at[i], chan=peer)
            cp.start()
            sent.append(cp)

    def from_groups(n, buf, ss, rs):
        for k in range(1, C):
            slot = buf.at[n, lax.rem(c + C - k, C)]
            i = n * (C - 1) + k - 1
            remote(slot, slot, ss.at[i], rs.at[i], chan=lax.rem(c + k, C)).wait_recv()

    mask = same_patch(T, T, patches)
    mask2 = same_patch(T, C * patches, patches)

    def forward(n):
        for j in range(3):
            if square:
                for slot in (3, 4, 5):
                    took(slot, j)
            own1[:, :FG] = jnp.zeros((T, FG), F32)

            def project(i, carry):
                rows = pl.ds(pl.multiple_of(i * W, W), W)
                own1[:, :FG] += mm(normed[i], wall[n, j, rows, :], NN)
                return carry

            lax.fori_loop(0, H, project, 0)
            proj[n, j] = own1[:, :FG].astype(BF16)
        for e in range(heads):
            cols = slice(e * HDIM, (e + 1) * HDIM)
            whole = slice(n * FG + e * HDIM, n * FG + (e + 1) * HDIM)
            qn, _ = unit(proj[n, 0][:, cols].astype(F32))
            kn, _ = unit(proj[n, 1][:, cols].astype(F32))
            w = softmax(qn, kn, mask)
            wts[n, e] = w
            first = mm(w.astype(BF16), proj[n, 2][:, cols], NN)
            own2[:, whole] = first
            mean = jnp.mean(first.reshape(chg, patches, HDIM), axis=0)
            own1[:patches, cols] = mean.astype(BF16).astype(F32)
        aggs[n, c] = own1[:patches, :FG]
        to_groups(n, lambda peer: aggs.at[n, c], aggs, as_, ar)

    def across(n):
        from_groups(n, aggs, as_, ar)
        for e in range(heads):
            cols = slice(e * HDIM, (e + 1) * HDIM)
            whole = slice(n * FG + e * HDIM, n * FG + (e + 1) * HDIM)
            a = aggs[n][:, :, cols].reshape(C * patches, HDIM)
            a16 = a.astype(BF16)
            qn, rq = unit(proj[n, 0][:, cols].astype(F32))
            an, ra = unit(a)
            w = softmax(qn, an, mask2)
            w16 = w.astype(BF16)
            own2[:, whole] += mm(w16, a16, NN)
            g16 = gm[:, whole].astype(BF16)
            dw = mm(g16, a16, NT)
            ds = w * (dw - jnp.sum(w * dw, axis=-1, keepdims=True)) * HDIM ** (-0.5)
            ds16 = ds.astype(BF16)
            gq2[:, whole] = unit_back(qn, rq, mm(ds16, an.astype(BF16), NN))
            da = mm(w16, g16, TN) + unit_back(an, ra, mm(ds16, qn.astype(BF16), TN))
            gsend[n, :, :, cols] = da.reshape(C, patches, HDIM)
        to_groups(n, lambda peer: gsend.at[n, peer], grecv, gas, gar)
        grecv[n, c] = gsend[n, c]

    def within(n):
        from_groups(n, grecv, gas, gar)
        back = grecv[n, 0]
        for i in range(1, C):
            back = back + grecv[n, i]
        back = back / chg
        for e in range(heads):
            cols = slice(e * HDIM, (e + 1) * HDIM)
            whole = slice(n * FG + e * HDIM, n * FG + (e + 1) * HDIM)
            lift = jnp.broadcast_to(back[None, :, cols], (chg, patches, HDIM)).reshape(T, HDIM)
            g16 = (gm[:, whole] + lift).astype(BF16)
            qn, rq = unit(proj[n, 0][:, cols].astype(F32))
            kn, rk = unit(proj[n, 1][:, cols].astype(F32))
            w = wts[n, e]
            dw = mm(g16, proj[n, 2][:, cols], NT)
            ds = w * (dw - jnp.sum(w * dw, axis=-1, keepdims=True)) * HDIM ** (-0.5)
            ds16 = ds.astype(BF16)
            dq = unit_back(qn, rq, mm(ds16, kn.astype(BF16), NN)) + gq2[:, whole]
            dk = unit_back(kn, rk, mm(ds16, qn.astype(BF16), TN))
            grads[0, :, cols] = dq.astype(BF16)
            grads[1, :, cols] = dk.astype(BF16)
            grads[2, :, cols] = mm(w.astype(BF16), g16, TN).astype(BF16)

    def back_proj(n, block):
        rows = pl.ds(pl.multiple_of(block * W, W), W)
        total = mm(grads[0], wall[n, 0, rows, :], NT)
        total += mm(grads[1], wall[n, 1, rows, :], NT)
        return total + mm(grads[2], wall[n, 2, rows, :], NT)

    if square:
        pass_on(0, 1)
        pass_on(1, 1)
    for cp in own_o:
        cp.wait()
    from_heads(call, cs, cr)
    gm[...] = jnp.zeros_like(gm)

    def mixed_block(i, carry):
        gm[...] += mm(call[i], wo[i], NT)
        return carry

    if square:
        pass_on(0, 2)
        pass_on(1, 2)
    lax.fori_loop(0, H, mixed_block, 0)
    weights(0)
    forward(0)
    across(0)

    later = []

    def chain_copy(way, m, snd, rcv, ss, rs):
        i = way * (H - 1) + m
        peer = lax.rem(h + 1, H) if way == 0 else lax.rem(h + H - 1, H)
        return remote(snd.at[i], rcv.at[i], ss.at[i], rs.at[i], head=peer)

    def chain_step(m, share, snd, rcv, ss, rs):
        for way in range(2):
            d = H - 1 - m if way == 0 else m
            first = (h == 0) if way == 0 else (h == H - 1)
            sends = (h < d) if way == 0 else (h > d)
            i = way * (H - 1) + m
            cp = chain_copy(way, m, snd, rcv, ss, rs)

            @pl.when(jnp.logical_and(sends, jnp.logical_not(first)))
            def _():
                cp.wait_recv()
                snd[i] = (share[d] + rcv[i].astype(F32)).astype(BF16)
                cp.start()

            later.append((sends, cp))

    def chain_open(d, share, snd, rcv, ss, rs):
        for way in range(2):
            m = H - 1 - d if way == 0 else d
            if m > H - 2:
                continue
            i = way * (H - 1) + m
            first = (h == 0) if way == 0 else (h == H - 1)

            @pl.when(first)
            def _():
                snd[i] = share[d].astype(BF16)
                chain_copy(way, m, snd, rcv, ss, rs).start()

    def chain_end(share, snd, rcv, ss, rs, total):
        total[...] = share[h]
        for way in range(2):
            for m in range(H - 1):
                d = H - 1 - m if way == 0 else m
                i = way * (H - 1) + m

                @pl.when(h == d)
                def _():
                    chain_copy(way, m, snd, rcv, ss, rs).wait_recv()
                    total[...] += rcv[i].astype(F32)

    order = []
    for m in range((H + 1) // 2):
        order += [H - 1 - m] + ([m] if m != H - 1 - m else [])
    mixed = own2[:, :F].astype(BF16)
    two = (acc2, s2, r2, s2s, s2r)
    for k in range(1, H):
        peer = lax.rem(h + k, H)
        s1[k - 1] = mm(mixed, wo[peer], NN).astype(BF16)
        cp = remote(s1.at[k - 1], r1.at[k - 1], s1s.at[k - 1], s1r.at[k - 1], head=peer)
        cp.start()
        sent.append(cp)
    own1[...] = mm(mixed, wo[h], NN)
    within(0)

    dots = jnp.zeros((T, 1), F32)
    for d in order:
        part = back_proj(0, d)
        acc2[d] = part
        chain_open(d, *two)
        dots += jnp.sum(hall[d].astype(F32) * gall[d][:1, :] * part, axis=-1, keepdims=True)
    corr[...] = jnp.broadcast_to(dots, corr.shape)
    for k in range(1, H):
        cp = remote(corr, rcorr.at[k - 1], ks.at[k - 1], kr.at[k - 1], head=lax.rem(h + k, H))
        cp.start()
        sent.append(cp)
    for m in range(H - 1):
        chain_step(m, *two)
    for k in range(1, H):
        slot = r1.at[k - 1]
        remote(slot, slot, s1s.at[k - 1], s1r.at[k - 1], head=lax.rem(h + k, H)).wait_recv()
        own1[...] += r1[k - 1].astype(F32)
    lay_ref[...] = (hid[...].astype(F32) + own1[...]).astype(BF16).reshape(lay_ref.shape)
    for k in range(1, H):
        remote(rcorr.at[k - 1], rcorr.at[k - 1], ks.at[k - 1], kr.at[k - 1], head=lax.rem(h + k, H)).wait_recv()
        corr_k = rcorr[k - 1]
        dots += corr_k[:, :1]
    chain_end(*two, own2)
    ir = inv[:, :1]
    grad = ir * gain8[:1, :] * own2[...] - hid[...].astype(F32) * (ir * ir * ir * dots / (H * W))
    inp_ref[...] = (cot[...].astype(F32) + grad).astype(BF16).reshape(inp_ref.shape)
    for cp in sent:
        cp.wait_send()
    for sends, cp in later:
        pl.when(sends)(cp.wait_send)


def per_device(C, H, R, tokens, position, gain, qkv_weight, out_weight, cotangent):
    channels, patches, W = tokens.shape
    T = channels * patches
    S, F = qkv_weight.shape[1:]
    G = 1
    FG = F // G
    heads = FG // HDIM
    D = S * C
    V = pltpu.VMEM
    dma = lambda n: pltpu.SemaphoreType.DMA((n,))
    nw = 18 if (C == 4 and R == 2) else G * (C - 1)
    z, g = H - 1, G * (C - 1)
    vm = pl.BlockSpec(memory_space=pltpu.VMEM)
    hbm = pl.BlockSpec(memory_space=pl.ANY)
    return pl.pallas_call(
        functools.partial(kernel, C, H, R, G),
        out_shape=[jax.ShapeDtypeStruct(tokens.shape, BF16)] * 2,
        in_specs=[vm, vm, vm, vm, hbm, hbm],
        out_specs=[vm, vm],
        scratch_shapes=[
            V((T, W), BF16), V((T, W), BF16), V((8, W), F32), V((H, T, W), F32), V((H, T, W), F32),
            V((G, 3, D, FG), BF16), V((H, F, W), BF16), V((H, T, W), BF16), V((H, T, W), BF16),
            V((H, 8, W), F32), V((H, T, W), BF16), V((T, HDIM), F32), V((G, 3, T, FG), BF16),
            V((T, F), F32), V((G, heads, T, T), F32), V((G, C, patches, FG), F32), V((T, F), F32),
            V((G, C, patches, FG), F32), V((G, C, patches, FG), F32), V((3, T, FG), BF16),
            V((2 * z, T, W), BF16), V((2 * z, T, W), BF16), V((2 * z, T, W), BF16), V((2 * z, T, W), BF16),
            V((T, W), F32), V((T, W), F32), V((T, HDIM), F32), V((z, T, HDIM), F32),
            dma(G + H), dma(nw), dma(nw), dma(z), dma(z), dma(z), dma(z), dma(z), dma(z),
            dma(g), dma(g), dma(g), dma(g), dma(2 * z), dma(2 * z), dma(2 * z), dma(2 * z), dma(z), dma(z),
        ],
        compiler_params=pltpu.CompilerParams(
            collective_id=0, has_side_effects=True, vmem_limit_bytes=50 * 1024 * 1024
        ),
    )(tokens, position, gain[None, :], cotangent, qkv_weight, out_weight)


def solution(mesh):
    C, H, R = (mesh.shape[a] for a in ("chan", "head", "region"))
    return jax.shard_map(
        functools.partial(per_device, C, H, R),
        mesh=mesh,
        in_specs=(
            P("chan", "region", "head"),
            P("chan", "head"),
            P("head"),
            P(None, "chan", "head"),
            P("head", None),
            P("chan", "region", "head"),
        ),
        out_specs=(P("chan", "region", "head"), P("chan", "region", "head")),
        check_vma=False,
    )
```
